512 devices in a mesh: ax: 16 (over z), xs: 32 (over x, y, core).
Axes of the slice: x: 4, y: 4, z: 16, core: 2. Of those that a mesh axis runs over, the one named last changes fastest.
Arguments:
- velocity: float32 [3, 128, 1024, 128], P(None, 'ax', 'xs'), may hold values from -6 to 6
- metric: float32 [3, 16, 128, 16], P(None, 'ax', 'xs'), may hold values from 0.05 to 0.3
- bubble_part: int32 [524288], P(('ax', 'xs')), may hold values from 0 to 31, as said below
- bubble_elem: int32 [524288], P(('ax', 'xs')), may hold values from 0 to 63
- bubble_ref: float32 [3, 524288], P(None, ('ax', 'xs')), may hold values from -1 to 1
- bubble_vel: float32 [3, 524288], P(None, ('ax', 'xs')), may hold values from -6 to 6
- inv_tau: float32 [524288], P(('ax', 'xs')), may hold values from 0.5 to 4
- basset_coef: float32 [524288], P(('ax', 'xs')), may hold values from 0.2 to 2
- history: bfloat16 [128, 3, 524288], P(None, None, ('ax', 'xs')), may hold values from -6 to 6
Outputs:
- fluid_rate: float32 [3, 128, 1024, 128], P(None, 'ax', 'xs')
- bubble_rate: float32 [3, 524288], P(None, ('ax', 'xs'))
The draws below stay inside these ranges and needn't reach their ends.
Inputs may be any that keep to these rules, and one draw needn't show every extreme that they name: `bubble_part`: among the bubbles of one holding device, at most 128 have their element in any one azimuthal sector; in each axial slab one sector holds the elements of exactly 128 bubbles of every device of that slab. `bubble_elem`: the index (ez 4 + ea) * 16 + er of the bubble's element inside its sector and its holder's slab.
All inputs are finite; a program needn't handle non-finite values.
Results may differ from the reference program's by a relative error of at most 0.0046.
Values sent between devices are 32-bit elements; how exact they have to be, the bound alone decides.
A program may use at most 64 MiB of HBM per device.

```python
import math
import jax
import jax.numpy as jnp
import numpy as np
from jax import lax

HIST = 128
EZ = 1
EA = 4
ER = 16
B_DEV = 1024
E_DEV = 64
EZN = 16
EAN = 128
ZN = 128
AN = 1024
RN = 128
BUBBLES = 524288
CAP = 128
N_AX = 16
N_XS = 32
DEVICES = 512


def draw_bubble_part(key, part):
    base = jax.random.fold_in(key, 7)
    full_key, order_key, shuffle_key = jax.random.split(base, 3)
    targets = jax.random.randint(full_key, (N_AX,), 0, N_XS)
    remaining = B_DEV - CAP
    places = jnp.arange(B_DEV)

    def one_device(device, order_seed, shuffle_seed):
        target = targets[device // N_XS]
        ranking = jax.random.permutation(order_seed, N_XS - 1)
        shifted = jnp.clip(places - CAP, 0, remaining - 1)
        others = (target + 1 + ranking[shifted * (N_XS - 1) // remaining]) % N_XS
        chosen = jnp.where(places < CAP, target, others)
        return jax.random.permutation(shuffle_seed, chosen)
    devices = jnp.arange(DEVICES)
    order_seeds = jax.random.split(order_key, DEVICES)
    shuffle_seeds = jax.random.split(shuffle_key, DEVICES)
    drawn = jax.vmap(one_device)(devices, order_seeds, shuffle_seeds)
    return drawn.reshape(-1).astype(jnp.int32)


def place_ends(values, own_key, least, high):
    place = [jax.random.randint(jax.random.fold_in(own_key, axis), (), 0, length) for axis, length in enumerate(values.shape)]
    main_axis = values.shape.index(max(values.shape))
    beside = place[:main_axis] + [(place[main_axis] + 1) % values.shape[main_axis]] + place[main_axis + 1:]
    return values.at[tuple(place)].set(least).at[tuple(beside)].set(high)


def levels(own_key, shape, shards, smallest, top_value):
    gain = 1.0
    for axis_at, blocks in shards:
        heights = jax.random.uniform(jax.random.fold_in(jax.random.fold_in(own_key, 6), axis_at), (blocks,), jnp.float32, smallest / len(shards), top_value / len(shards))
        gain = gain * jnp.repeat(jnp.exp(heights), shape[axis_at] // blocks).reshape((-1,) + (1,) * (len(shape) - 1 - axis_at))
    return gain


def scatter_about(rng, dims, scale, limit, shards=(), held_as=jnp.bfloat16):
    result = scale * jax.random.normal(rng, dims, jnp.float32)
    if shards:
        result = result * levels(rng, dims, shards, -0.22, 0.18)
    return jnp.clip(result, -limit, limit).astype(held_as)


def setup_inputs(seed: int = 0) -> dict:
    splits = jax.random.split(jax.random.key(seed), 10)
    velocity = scatter_about(splits[0], (3, ZN, AN, RN), 1.0, 6.0, ((1, 16), (2, 32)), jnp.float32)
    metric = jnp.clip(jnp.exp(math.log(0.3) - 1.7917595 * jax.random.uniform(splits[1], (3, EZN, EAN, ER), jnp.float32) ** levels(splits[1], (3, EZN, EAN, ER), ((1, 16), (2, 32)), -0.2, 0.2)), 0.05, 0.3)
    bubble_part = draw_bubble_part(jax.random.fold_in(splits[9], 71), 0)
    bubble_elem = place_ends(jax.random.randint(splits[3], (BUBBLES,), 0, E_DEV), jax.random.fold_in(splits[3], 1), 0, E_DEV - 1).astype(jnp.int32)
    bubble_ref = jnp.clip(jax.random.uniform(splits[4], (3, BUBBLES), jnp.float32, -1.0, 1.0) * levels(splits[4], (3, BUBBLES), ((1, 512),), -0.4, 0.0), -1.0, 1.0)
    bubble_vel = scatter_about(splits[5], (3, BUBBLES), 1.0, 6.0, ((1, 512),), jnp.float32)
    inv_tau = jnp.clip(jnp.exp(math.log(4.0) - 2.0794415 * jax.random.uniform(splits[6], (BUBBLES,), jnp.float32) ** levels(splits[6], (BUBBLES,), ((0, 512),), -0.2, 0.2)), 0.5, 4.0)
    basset_coef = jnp.clip(jnp.exp(math.log(2.0) - 2.3025851 * jax.random.uniform(splits[7], (BUBBLES,), jnp.float32) ** levels(splits[7], (BUBBLES,), ((0, 512),), -0.2, 0.2)), 0.2, 2.0)
    history = scatter_about(splits[8], (HIST, 3, BUBBLES), 1.0, 6.0, ((2, 512),))
    return {"velocity": velocity, "metric": metric, "bubble_part": bubble_part, "bubble_elem": bubble_elem, "bubble_ref": bubble_ref, "bubble_vel": bubble_vel, "inv_tau": inv_tau, "basset_coef": basset_coef, "history": history}


GLL_POINTS = (-1.0, -0.8717401485096066, -0.5917001814331423, -0.2092992179024789, 0.2092992179024789, 0.5917001814331423, 0.8717401485096066, 1.0)
GLL_WEIGHTS = (0.03571428571428571, 0.21070422714350603, 0.34112269248350435, 0.4124587946587039, 0.4124587946587039, 0.34112269248350435, 0.21070422714350603, 0.03571428571428571)

def derivative_matrix():
    points = np.array(GLL_POINTS)
    identity = np.eye(8)
    spread = points[:, None] - points[None, :] + identity
    products = np.prod(spread, axis=1)
    matrix = products[:, None] / products[None, :] / spread
    off_diagonal = matrix * (1.0 - identity)
    return off_diagonal - identity * off_diagonal.sum(axis=1)[:, None]

def lagrange_weights(coord):
    columns = []
    for node_index in range(8):
        factor = jnp.ones_like(coord)
        for other_node in range(8):
            if other_node != node_index:
                factor = factor * ((coord - GLL_POINTS[other_node]) / (GLL_POINTS[node_index] - GLL_POINTS[other_node]))
        columns.append(factor)
    return jnp.stack(columns, axis=0)

def expand_metric(metric):
    return jnp.repeat(jnp.repeat(jnp.repeat(metric, 8, axis=1), 8, axis=2), 8, axis=3)

def advection(velocity, scale):
    matrix = jnp.asarray(derivative_matrix(), jnp.float32)
    comps, zlength, alength, rlength = velocity.shape
    along_z = jnp.einsum('ij,czjar->cziar', matrix, velocity.reshape(comps, zlength // 8, 8, alength, rlength), precision=lax.Precision.HIGHEST).reshape(velocity.shape)
    along_a = jnp.einsum('ij,czajr->czair', matrix, velocity.reshape(comps, zlength, alength // 8, 8, rlength), precision=lax.Precision.HIGHEST).reshape(velocity.shape)
    radial_matrix = jnp.asarray(np.kron(np.eye(rlength // 8), derivative_matrix().T), jnp.float32)
    along_r = jnp.dot(velocity, radial_matrix, precision=lax.Precision.HIGHEST)
    return velocity[0:1] * scale[0:1] * along_z + velocity[1:2] * scale[1:2] * along_a + velocity[2:3] * scale[2:3] * along_r

def nodal_mass(scale):
    weights = np.array(GLL_WEIGHTS)
    zlength, alength, rlength = scale.shape[1:]
    weight_z = jnp.asarray(np.tile(weights, zlength // 8), jnp.float32)
    weight_a = jnp.asarray(np.tile(weights, alength // 8), jnp.float32)
    weight_r = jnp.asarray(np.tile(weights, rlength // 8), jnp.float32)
    return weight_z[:, None, None] * weight_a[None, :, None] * weight_r[None, None, :] / (scale[0] * scale[1] * scale[2])

def pair_sum(values, axis_dim, periodic):
    length = values.shape[axis_dim]
    shape = [1] * values.ndim
    shape[axis_dim] = length
    places = jnp.arange(length).reshape(shape)
    after = jnp.roll(values, -1, axis_dim)
    before = jnp.roll(values, 1, axis_dim)
    upper = places % 8 == 7
    lower = places % 8 == 0
    if not periodic:
        upper = upper & (places < length - 1)
        lower = lower & (places > 0)
    return values + jnp.where(upper, after, 0.0) + jnp.where(lower, before, 0.0)

def interpolate(rows, coords):
    lag_z = lagrange_weights(coords[0]).astype(jnp.bfloat16).astype(jnp.float32)
    lag_a = lagrange_weights(coords[1]).astype(jnp.bfloat16).astype(jnp.float32)
    lag_r = lagrange_weights(coords[2]).astype(jnp.bfloat16).astype(jnp.float32)
    slots = rows.shape[0]
    first = jnp.einsum('sxr,rs->sx', rows.reshape(slots, -1, 8), lag_r, precision=lax.Precision.HIGHEST)
    second = jnp.einsum('sxa,as->sx', first.reshape(slots, -1, 8), lag_a, precision=lax.Precision.HIGHEST)
    return jnp.einsum('scz,zs->cs', second.reshape(slots, -1, 8), lag_z, precision=lax.Precision.HIGHEST)

def quadrature(length):
    steps = jnp.arange(length).astype(jnp.float32)
    return (jnp.sqrt(steps + 1.0) - jnp.sqrt(steps)).astype(jnp.bfloat16)

def reference(velocity, metric, bubble_part, bubble_elem, bubble_ref, bubble_vel, inv_tau, basset_coef, history):
    scale = expand_metric(metric)
    advect = advection(velocity, scale)
    mass = nodal_mass(scale)
    weighted = jnp.concatenate([mass[None] * advect, mass[None]], axis=0)
    summed = pair_sum(weighted, 3, False)
    summed = pair_sum(summed, 2, True)
    summed = pair_sum(summed, 1, True)
    fluid_rate = -summed[0:3] / summed[3:4]
    source = jnp.concatenate([velocity, advect], axis=0).astype(jnp.bfloat16)
    quad = quadrature(HIST)
    basset = basset_coef[None] * jnp.dot(quad, history.reshape(HIST, -1), preferred_element_type=jnp.float32).reshape(3, BUBBLES)
    block = B_DEV * 8
    blocks = BUBBLES // block
    positions = jnp.arange(BUBBLES).astype(jnp.int32)

    def one_block(inputs):
        part_block, elem_block, coord_block, index_block = inputs
        slab = index_block // B_DEV // N_XS
        z_start = (8 * (slab * EZ + elem_block // (EA * ER))).astype(jnp.int32)
        a_start = (8 * (part_block * EA + elem_block // ER % EA)).astype(jnp.int32)
        r_start = (8 * (elem_block % ER)).astype(jnp.int32)

        def cut(z_first, a_first, r_first):
            return lax.dynamic_slice(source, (jnp.int32(0), z_first, a_first, r_first), (6, 8, 8, 8)).reshape(-1)
        rows = jax.vmap(cut)(z_start, a_start, r_start).astype(jnp.float32)
        return interpolate(rows, coord_block)
    probes = lax.map(one_block, (bubble_part.reshape(blocks, block), bubble_elem.reshape(blocks, block), jnp.moveaxis(bubble_ref.reshape(3, blocks, block), 1, 0), positions.reshape(blocks, block)))
    probe = jnp.moveaxis(probes, 0, 1).reshape(6, BUBBLES)
    bubble_rate = 3.0 * probe[3:6] + inv_tau[None] * (probe[0:3] - bubble_vel) + basset
    return (fluid_rate, bubble_rate)
```

```python
import functools

import jax
import jax.numpy as jnp
import numpy as np
from jax import lax
from jax.experimental import pallas as pl
from jax.experimental.pallas import tpu as pltpu
from jax.sharding import PartitionSpec as P

GLL_POINTS = (
    -1.0,
    -0.8717401485096066,
    -0.5917001814331423,
    -0.2092992179024789,
    0.2092992179024789,
    0.5917001814331423,
    0.8717401485096066,
    1.0,
)
GLL_WEIGHTS = (
    0.03571428571428571,
    0.21070422714350603,
    0.34112269248350435,
    0.4124587946587039,
    0.4124587946587039,
    0.34112269248350435,
    0.21070422714350603,
    0.03571428571428571,
)
SLOTS = 128
MESH = pl.DeviceIdType.MESH
F32 = jnp.float32
BF16 = jnp.bfloat16


def derivative_matrix():
    points = np.array(GLL_POINTS)
    identity = np.eye(8)
    spread = points[:, None] - points[None, :] + identity
    products = np.prod(spread, axis=1)
    matrix = products[:, None] / products[None, :] / spread
    off_diagonal = matrix * (1.0 - identity)
    return off_diagonal - identity * off_diagonal.sum(axis=1)[:, None]


DMAT = derivative_matrix()

ROW_POINT = 0
ROW_NORM = 8
ROW_ROLL = 16
ROW_WEIGHT = 80
ROW_RADIAL = 112


def constant_table():
    points = np.array(GLL_POINTS)
    weights = np.array(GLL_WEIGHTS)
    rows = [np.repeat(points[:, None], 128, axis=1)]
    spread = points[:, None] - points[None, :] + np.eye(8)
    rows.append(np.repeat((1.0 / np.prod(spread, axis=1))[:, None], 128, axis=1))
    for shift in range(8):
        coef = np.array([DMAT[i, (i - shift) % 8] for i in range(8)])
        rows.append(np.repeat(coef[:, None], 128, axis=1))
    rows.append(np.tile(weights, 4)[:, None] * np.tile(weights, 16)[None, :])
    rows.append(np.kron(np.eye(16), DMAT.T))
    return np.concatenate(rows, axis=0).astype(np.float32)


def quadrature_rows(length):
    steps = np.arange(length, dtype=np.float32)
    quad = np.sqrt(steps + np.float32(1.0)) - np.sqrt(steps)
    rows = np.zeros((16, length, 3), np.float32)
    for comp in range(3):
        rows[comp, :, comp] = quad
    return rows.reshape(16, length * 3)


def split3(values):
    high = values.astype(BF16).astype(F32)
    rest = values - high
    mid = rest.astype(BF16).astype(F32)
    return high, mid, rest - mid


def kernel(
    n_ax, n_xs,
    vel_ref, scale_ref, part_ref, elem_ref, ref_ref, bvel_ref, tau_ref, coef_ref,
    hist_ref, const_ref, quad_ref,
    fluid_ref, bubble_ref,
    hist_buf, lhs, onehot, sendq, recvq, sendr, recvr, table, wsum, weights_za,
    face_out, face_in, plane_out, plane_in,
    local_sem, q_send, q_recv, r_send, r_recv, h_send, h_recv,
):
    ax = lax.axis_index("ax")
    me = lax.axis_index("xs")
    held = part_ref.shape[1]

    barrier = pltpu.get_barrier_semaphore()

    def greet(step, carry):
        pl.semaphore_signal(
            barrier, inc=1, device_id=(ax, lax.rem(me + step, n_xs)), device_id_type=MESH
        )
        return carry

    lax.fori_loop(1, n_xs, greet, 0)
    up, down = lax.rem(ax + 1, n_ax), lax.rem(ax + n_ax - 1, n_ax)
    for other in (up, down):
        pl.semaphore_signal(barrier, inc=1, device_id=(other, me), device_id_type=MESH)

    load_hist = pltpu.make_async_copy(hist_ref, hist_buf, local_sem)
    load_hist.start()

    rel = part_ref[...] - me
    rel = jnp.where(rel < 0, rel + n_xs, rel)
    member = (
        jnp.broadcast_to(rel, (n_xs, held))
        == lax.broadcasted_iota(jnp.int32, (n_xs, held), 0)
    ).astype(F32)
    chunks = held // 128
    pieces = [member[:, c * 128 : (c + 1) * 128] for c in range(chunks)]
    stacked = jnp.concatenate(pieces, axis=0).astype(BF16)
    before = (
        lax.broadcasted_iota(jnp.int32, (128, 128), 0)
        < lax.broadcasted_iota(jnp.int32, (128, 128), 1)
    ).astype(F32).astype(BF16)
    counts = jnp.dot(stacked, before, preferred_element_type=F32)
    totals = jnp.dot(stacked, jnp.ones((128, 128), BF16), preferred_element_type=F32)
    carry = jnp.zeros((n_xs, 128), F32)
    ranks = []
    for c in range(chunks):
        rows = slice(c * n_xs, (c + 1) * n_xs)
        ranks.append(jnp.sum(pieces[c] * (counts[rows] + carry), axis=0, keepdims=True))
        carry = carry + totals[rows]
    rank = jnp.concatenate(ranks, axis=1).astype(jnp.int32)
    onehot[...] = (
        jnp.broadcast_to(rank, (SLOTS, held))
        == lax.broadcasted_iota(jnp.int32, (SLOTS, held), 0)
    ).astype(F32).astype(BF16)

    query = jnp.concatenate(
        [ref_ref[...], elem_ref[...].astype(F32), tau_ref[...], jnp.zeros((3, held), F32)],
        axis=0,
    )
    parts = split3(query)
    rel8 = jnp.broadcast_to(rel, (8, held))
    span = 8 * n_xs

    for which in range(3):
        for step in range(0, n_xs, 2):
            pair = jnp.concatenate(
                [jnp.where(rel8 == step + i, parts[which], 0.0) for i in range(2)], axis=0
            )
            lhs[which * span + 8 * step : which * span + 8 * step + 16, :] = pair.astype(BF16)
    slots = lax.dot_general(
        lhs[...], onehot[...], (((1,), (1,)), ((), ())), preferred_element_type=F32
    )
    slots = slots[:span] + slots[span : 2 * span] + slots[2 * span :]
    slots = slots.reshape(n_xs, 8, SLOTS)
    sendq[...] = slots
    recvq[0] = slots[0]

    pl.semaphore_wait(barrier, n_xs + 1)

    def query_copy(step, target):
        return pltpu.make_async_remote_copy(
            src_ref=sendq.at[step, pl.ds(0, 5)],
            dst_ref=recvq.at[step, pl.ds(0, 5)],
            send_sem=q_send.at[step],
            recv_sem=q_recv.at[step],
            device_id=(ax, target),
            device_id_type=MESH,
        )

    def send_query(step, carry):
        query_copy(step, lax.rem(me + step, n_xs)).start()
        return carry

    lax.fori_loop(1, n_xs, send_query, 0)

    vel = vel_ref[...]
    length_a, length_r = vel.shape[2], vel.shape[3]
    nodes = 8 * length_a
    grad_r = jnp.dot(
        vel.reshape(3 * nodes, length_r),
        const_ref[ROW_RADIAL : ROW_RADIAL + 128, :],
        preferred_element_type=F32,
        precision=lax.Precision.HIGHEST,
    ).reshape(vel.shape)
    scale = scale_ref[...]
    inverse = const_ref[ROW_WEIGHT : ROW_WEIGHT + 32, :] / (scale[0] * scale[1] * scale[2])
    lane = lax.broadcasted_iota(jnp.int32, (4, length_a, length_r), 2)
    upper = (lane % 8 == 7) & (lane < length_r - 1)
    lower = (lane % 8 == 0) & (lane > 0)
    for z in range(8):
        here = vel[:, z]
        grad_z = sum(float(DMAT[z, j]) * vel[:, j] for j in range(8) if abs(DMAT[z, j]) > 1e-9)
        groups = here.reshape(3 * length_a // 8, 8, length_r)
        grad_a = const_ref[ROW_ROLL : ROW_ROLL + 8, :] * groups
        for shift in range(1, 8):
            coef = const_ref[ROW_ROLL + 8 * shift : ROW_ROLL + 8 * shift + 8, :]
            grad_a = grad_a + coef * pltpu.roll(groups, shift, 1)
        grad_a = grad_a.reshape(here.shape)
        advect = (
            (here[0] * scale[0])[None] * grad_z
            + (here[1] * scale[1])[None] * grad_a
            + (here[2] * scale[2])[None] * grad_r[:, z]
        )
        for comp in range(3):
            row = comp * nodes + z * length_a
            table[row : row + length_a, :] = here[comp].astype(BF16)
            row = row + 3 * nodes
            table[row : row + length_a, :] = advect[comp].astype(BF16)
        mass = GLL_WEIGHTS[z] * inverse
        weighted = jnp.concatenate([mass[None] * advect, mass[None]], axis=0)
        after = pltpu.roll(weighted, length_r - 1, 2)
        prior = pltpu.roll(weighted, 1, 2)
        wsum[:, z] = weighted + jnp.where(upper, after, jnp.where(lower, prior, 0.0))

    for edge in range(8, length_a, 8):
        both = wsum[:, :, edge - 1 : edge, :] + wsum[:, :, edge : edge + 1, :]
        wsum[:, :, edge - 1 : edge, :] = both
        wsum[:, :, edge : edge + 1, :] = both
    for z in range(8):
        face_out[0, :, z : z + 1, :] = wsum[:, z, length_a - 1 : length_a, :]
        face_out[1, :, z : z + 1, :] = wsum[:, z, 0:1, :]

    def face_copy(side):
        target = lax.rem(me + (1 if side == 0 else n_xs - 1), n_xs)
        return pltpu.make_async_remote_copy(
            src_ref=face_out.at[side],
            dst_ref=face_in.at[side],
            send_sem=h_send.at[side],
            recv_sem=h_recv.at[side],
            device_id=(ax, target),
            device_id_type=MESH,
        )

    def plane_copy(side):
        return pltpu.make_async_remote_copy(
            src_ref=plane_out.at[side],
            dst_ref=plane_in.at[side],
            send_sem=h_send.at[2 + side],
            recv_sem=h_recv.at[2 + side],
            device_id=(up if side == 0 else down, me),
            device_id_type=MESH,
        )

    faces = [face_copy(side) for side in range(2)]
    for face in faces:
        face.start()

    load_hist.wait()
    basset = jnp.dot(quad_ref[...], hist_buf[...], preferred_element_type=F32)[0:3]
    local = coef_ref[...] * basset - tau_ref[...] * bvel_ref[...]

    faces[0].wait()
    faces[1].wait()
    for z in range(8):
        wsum[:, z, 0:1, :] = wsum[:, z, 0:1, :] + face_in[0, :, z : z + 1, :]
        last = slice(length_a - 1, length_a)
        wsum[:, z, last, :] = wsum[:, z, last, :] + face_in[1, :, z : z + 1, :]
    plane_out[0] = wsum[:, 7]
    plane_out[1] = wsum[:, 0]
    planes = [plane_copy(side) for side in range(2)]
    for plane in planes:
        plane.start()

    def answer_copy(step):
        return pltpu.make_async_remote_copy(
            src_ref=sendr.at[step, pl.ds(0, 3)],
            dst_ref=recvr.at[step, pl.ds(0, 3)],
            send_sem=r_send.at[step],
            recv_sem=r_recv.at[step],
            device_id=(ax, lax.rem(me + n_xs - step, n_xs)),
            device_id_type=MESH,
        )

    point = jnp.concatenate([const_ref[ROW_POINT : ROW_POINT + 8, :]] * 2, axis=1)
    norm = jnp.concatenate([const_ref[ROW_NORM : ROW_NORM + 8, :]] * 2, axis=1)

    def lagrange(row):
        diff = row - point
        one = pltpu.roll(diff, 1, 0)
        two = one * pltpu.roll(one, 1, 0)
        four = two * pltpu.roll(two, 2, 0)
        rest = four * pltpu.roll(two, 4, 0) * pltpu.roll(one, 6, 0)
        return (rest * norm).astype(BF16).astype(F32)

    def serve(pair, carry):
        first_step = 2 * pair

        @pl.when(pair > 0)
        def _():
            query_copy(first_step, me).wait_recv()

        query_copy(first_step + 1, me).wait_recv()
        both = jnp.concatenate([recvq[first_step], recvq[first_step + 1]], axis=1)
        lag_z = lagrange(both[0:1])
        lag_a = lagrange(both[1:2])
        lag_r = lagrange(both[2:3])
        element = both[3:4].astype(jnp.int32)
        radial = jnp.broadcast_to(element & 15, (8, 2 * SLOTS))
        azimuth = jnp.broadcast_to((element >> 4) & 3, (8, 2 * SLOTS))
        tau = both[4:5]
        weight_r = jnp.concatenate(
            [jnp.where(radial == e, lag_r, 0.0) for e in range(length_r // 8)], axis=0
        ).astype(BF16)
        masked = jnp.concatenate(
            [jnp.where(azimuth == e, lag_a, 0.0) for e in range(length_a // 8)], axis=0
        )
        for z in range(8):
            weights_za[z * length_a : (z + 1) * length_a, :] = lag_z[z : z + 1] * masked
        sums = []
        for field in range(6):
            first = jnp.dot(
                table[field * nodes : (field + 1) * nodes, :],
                weight_r,
                preferred_element_type=F32,
            )
            product = (first * weights_za[...]).reshape(nodes // 8, 8, 2 * SLOTS)
            sums.append(jnp.sum(product, axis=0))
        for comp in range(3):
            value = jnp.sum(3.0 * sums[3 + comp] + tau * sums[comp], axis=0, keepdims=True)
            sendr[first_step, comp : comp + 1, :] = value[:, :SLOTS]
            sendr[first_step + 1, comp : comp + 1, :] = value[:, SLOTS:]

        @pl.when(pair > 0)
        def _():
            answer_copy(first_step).start()

        answer_copy(first_step + 1).start()
        return carry

    lax.fori_loop(0, n_xs // 2, serve, 0)

    planes[0].wait()
    planes[1].wait()
    for z in range(8):
        total = wsum[:, z]
        if z == 0:
            total = total + plane_in[0]
        if z == 7:
            total = total + plane_in[1]
        fluid_ref[:, z] = total[0:3] * (-1.0 / total[3:4])

    recvr[0, 0:3] = sendr[0, 0:3]

    def finish(step, carry):
        query_copy(step, me).wait_send()
        answer_copy(step).wait()
        return carry

    lax.fori_loop(1, n_xs, finish, 0)

    answers = recvr[...].reshape(span, SLOTS)
    spread = jnp.dot(
        jnp.concatenate([p.astype(BF16) for p in split3(answers)], axis=0),
        onehot[...],
        preferred_element_type=F32,
    )
    total = jnp.zeros((8, held), F32)
    for step in range(n_xs):
        rows = [spread[w * span + 8 * step : w * span + 8 * step + 8] for w in range(3)]
        total = total + jnp.where(rel8 == step, rows[0] + rows[1] + rows[2], 0.0)
    bubble_ref[...] = total[0:3] + local


def shards(
    velocity, metric, bubble_part, bubble_elem, bubble_ref, bubble_vel, inv_tau,
    basset_coef, history,
):
    n_ax, n_xs = lax.axis_size("ax"), lax.axis_size("xs")
    held = bubble_part.shape[0]
    steps = history.shape[0]
    _, length_z, length_a, length_r = velocity.shape
    scale = jnp.repeat(jnp.repeat(metric[:, 0], 8, axis=1), 8, axis=2)
    const = jnp.asarray(constant_table())
    quad = jnp.asarray(quadrature_rows(steps), BF16)
    nodes = length_z * length_a
    vmem = pl.BlockSpec(memory_space=pltpu.VMEM)
    anywhere = pl.BlockSpec(memory_space=pl.ANY)
    dma = pltpu.SemaphoreType.DMA
    return pl.pallas_call(
        functools.partial(kernel, n_ax, n_xs),
        out_shape=(
            jax.ShapeDtypeStruct(velocity.shape, F32),
            jax.ShapeDtypeStruct((3, held), F32),
        ),
        in_specs=[vmem] * 8 + [anywhere] + [vmem] * 2,
        out_specs=(vmem, vmem),
        scratch_shapes=[
            pltpu.VMEM((3 * steps, held), BF16),
            pltpu.VMEM((3 * 8 * n_xs, held), BF16),
            pltpu.VMEM((SLOTS, held), BF16),
            pltpu.VMEM((n_xs, 8, SLOTS), F32),
            pltpu.VMEM((n_xs, 8, SLOTS), F32),
            pltpu.VMEM((n_xs, 8, SLOTS), F32),
            pltpu.VMEM((n_xs, 8, SLOTS), F32),
            pltpu.VMEM((6 * nodes, length_r), BF16),
            pltpu.VMEM((4, length_z, length_a, length_r), F32),
            pltpu.VMEM((nodes, 2 * SLOTS), F32),
            pltpu.VMEM((2, 4, length_z, length_r), F32),
            pltpu.VMEM((2, 4, length_z, length_r), F32),
            pltpu.VMEM((2, 4, length_a, length_r), F32),
            pltpu.VMEM((2, 4, length_a, length_r), F32),
            dma,
            dma((n_xs,)),
            dma((n_xs,)),
            dma((n_xs,)),
            dma((n_xs,)),
            dma((4,)),
            dma((4,)),
        ],
        compiler_params=pltpu.CompilerParams(
            collective_id=0, has_side_effects=True, vmem_limit_bytes=40 * 1024 * 1024
        ),
    )(
        velocity,
        scale,
        bubble_part.reshape(1, held),
        bubble_elem.reshape(1, held),
        bubble_ref,
        bubble_vel,
        inv_tau.reshape(1, held),
        basset_coef.reshape(1, held),
        history.reshape(3 * steps, held),
        const,
        quad,
    )


def solution(mesh):
    return jax.shard_map(
        shards,
        mesh=mesh,
        in_specs=(
            P(None, "ax", "xs", None),
            P(None, "ax", "xs", None),
            P(("ax", "xs")),
            P(("ax", "xs")),
            P(None, ("ax", "xs")),
            P(None, ("ax", "xs")),
            P(("ax", "xs")),
            P(("ax", "xs")),
            P(None, None, ("ax", "xs")),
        ),
        out_specs=(P(None, "ax", "xs", None), P(None, ("ax", "xs"))),
        check_vma=False,
    )
```

```python
import functools

import jax
import jax.numpy as jnp
import numpy as np
from jax import lax
from jax.experimental import pallas as pl
from jax.experimental.pallas import tpu as pltpu
from jax.sharding import PartitionSpec as P

GLL_POINTS = (
    -1.0,
    -0.8717401485096066,
    -0.5917001814331423,
    -0.2092992179024789,
    0.2092992179024789,
    0.5917001814331423,
    0.8717401485096066,
    1.0,
)
GLL_WEIGHTS = (
    0.03571428571428571,
    0.21070422714350603,
    0.34112269248350435,
    0.4124587946587039,
    0.4124587946587039,
    0.34112269248350435,
    0.21070422714350603,
    0.03571428571428571,
)
SLOTS = 128
GROUP = 4
MESH = pl.DeviceIdType.MESH
F32 = jnp.float32
BF16 = jnp.bfloat16


def derivative_matrix():
    points = np.array(GLL_POINTS)
    identity = np.eye(8)
    spread = points[:, None] - points[None, :] + identity
    products = np.prod(spread, axis=1)
    matrix = products[:, None] / products[None, :] / spread
    off_diagonal = matrix * (1.0 - identity)
    return off_diagonal - identity * off_diagonal.sum(axis=1)[:, None]


DMAT = derivative_matrix()

ROW_POINT = 0
ROW_NORM = 8
ROW_ROLL = 16
ROW_WEIGHT = 80
ROW_RADIAL = 112


def constant_table():
    points = np.array(GLL_POINTS)
    weights = np.array(GLL_WEIGHTS)
    rows = [np.repeat(points[:, None], 128, axis=1)]
    spread = points[:, None] - points[None, :] + np.eye(8)
    rows.append(np.repeat((1.0 / np.prod(spread, axis=1))[:, None], 128, axis=1))
    for shift in range(8):
        coef = np.array([DMAT[i, (i - shift) % 8] for i in range(8)])
        rows.append(np.repeat(coef[:, None], 128, axis=1))
    rows.append(np.tile(weights, 4)[:, None] * np.tile(weights, 16)[None, :])
    rows.append(np.kron(np.eye(16), DMAT.T))
    return np.concatenate(rows, axis=0).astype(np.float32)


def quadrature_rows(length):
    steps = np.arange(length, dtype=np.float32)
    quad = np.sqrt(steps + np.float32(1.0)) - np.sqrt(steps)
    rows = np.zeros((16, 3, length), np.float32)
    for comp in range(3):
        rows[comp, comp] = quad
    return rows.reshape(16, 3 * length)


def split3(values):
    high = values.astype(BF16).astype(F32)
    rest = values - high
    mid = rest.astype(BF16).astype(F32)
    return high, mid, rest - mid


def ranked(rel, n_xs, onehot):
    held = rel.shape[1]
    member = (
        jnp.broadcast_to(rel, (n_xs, held))
        == lax.broadcasted_iota(jnp.int32, (n_xs, held), 0)
    ).astype(F32)
    chunks = held // 128
    pieces = [member[:, c * 128 : (c + 1) * 128] for c in range(chunks)]
    stacked = jnp.concatenate(pieces, axis=0).astype(BF16)
    before = (
        lax.broadcasted_iota(jnp.int32, (128, 128), 0)
        < lax.broadcasted_iota(jnp.int32, (128, 128), 1)
    ).astype(F32).astype(BF16)
    counts = jnp.dot(stacked, before, preferred_element_type=F32)
    totals = jnp.dot(stacked, jnp.ones((128, 128), BF16), preferred_element_type=F32)
    carry = jnp.zeros((n_xs, 128), F32)
    ranks = []
    for c in range(chunks):
        rows = slice(c * n_xs, (c + 1) * n_xs)
        ranks.append(jnp.sum(pieces[c] * (counts[rows] + carry), axis=0, keepdims=True))
        carry = carry + totals[rows]
    rank = jnp.concatenate(ranks, axis=1).astype(jnp.int32)
    onehot[...] = (
        jnp.broadcast_to(rank, (SLOTS, held))
        == lax.broadcasted_iota(jnp.int32, (SLOTS, held), 0)
    ).astype(F32).astype(BF16)


def dispatch(rel, n_xs, coords, elem, lhs, onehot, sendq, recvq):
    held = rel.shape[1]
    high, mid, low = split3(coords)
    packed = jnp.concatenate(
        [high, elem, jnp.zeros((3, held), F32), mid, low], axis=0
    ).astype(BF16)
    rel16 = jnp.broadcast_to(rel, (16, held))
    zero = jnp.zeros((16, held), BF16)
    for step in range(n_xs):
        lhs[16 * step : 16 * step + 16, :] = jnp.where(rel16 == step, packed, zero)
    slots = lax.dot_general(
        lhs[...], onehot[...], (((1,), (1,)), ((), ())), preferred_element_type=F32
    ).reshape(n_xs, 2, 8, SLOTS)
    rest = slots[:, 1]
    rest = rest + pltpu.roll(rest, 4, 1)
    row = lax.broadcasted_iota(jnp.int32, (n_xs, 8, SLOTS), 1)
    slots = slots[:, 0] + jnp.where(row < 4, rest, 0.0)
    sendq[...] = slots
    recvq[0] = slots[0]


def advection(vel_ref, scale_ref, const_ref, table, wsum):
    vel = vel_ref[...]
    length_a, length_r = vel.shape[2], vel.shape[3]
    nodes = 8 * length_a
    grad_r = jnp.dot(
        vel.reshape(3 * nodes, length_r),
        const_ref[ROW_RADIAL : ROW_RADIAL + 128, :],
        preferred_element_type=F32,
        precision=lax.Precision.HIGHEST,
    ).reshape(vel.shape)
    scale = scale_ref[...]
    inverse = const_ref[ROW_WEIGHT : ROW_WEIGHT + 32, :] / (scale[0] * scale[1] * scale[2])
    lane = lax.broadcasted_iota(jnp.int32, (4, length_a, length_r), 2)
    upper = (lane % 8 == 7) & (lane < length_r - 1)
    lower = (lane % 8 == 0) & (lane > 0)
    for z in range(8):
        here = vel[:, z]
        grad_z = sum(float(DMAT[z, j]) * vel[:, j] for j in range(8) if abs(DMAT[z, j]) > 1e-9)
        groups = here.reshape(3 * length_a // 8, 8, length_r)
        grad_a = const_ref[ROW_ROLL : ROW_ROLL + 8, :] * groups
        for shift in range(1, 8):
            coef = const_ref[ROW_ROLL + 8 * shift : ROW_ROLL + 8 * shift + 8, :]
            grad_a = grad_a + coef * pltpu.roll(groups, shift, 1)
        grad_a = grad_a.reshape(here.shape)
        advect = (
            (here[0] * scale[0])[None] * grad_z
            + (here[1] * scale[1])[None] * grad_a
            + (here[2] * scale[2])[None] * grad_r[:, z]
        )
        fields = [here[0], here[1], here[2], advect[0], advect[1], advect[2]]
        if z % 2 == 1:
            for field in range(6):
                for element in range(length_a // 8):
                    rows = slice(8 * element, 8 * element + 8)
                    pair = jnp.concatenate([earlier[field][rows], fields[field][rows]], axis=0)
                    table[
                        64 * field + 8 * (z - 1) : 64 * field + 8 * (z + 1),
                        length_r * element : length_r * (element + 1),
                    ] = pair.astype(BF16)
        earlier = fields
        mass = GLL_WEIGHTS[z] * inverse
        weighted = jnp.concatenate([mass[None] * advect, mass[None]], axis=0)
        after = pltpu.roll(weighted, length_r - 1, 2)
        prior = pltpu.roll(weighted, 1, 2)
        wsum[:, z] = weighted + jnp.where(upper, after, jnp.where(lower, prior, 0.0))


def azimuth_pairs(wsum, face_out):
    length_a = wsum.shape[2]
    for edge in range(8, length_a, 8):
        both = wsum[:, :, edge - 1 : edge, :] + wsum[:, :, edge : edge + 1, :]
        wsum[:, :, edge - 1 : edge, :] = both
        wsum[:, :, edge : edge + 1, :] = both
    for z in range(8):
        face_out[0, :, z : z + 1, :] = wsum[:, z, length_a - 1 : length_a, :]
        face_out[1, :, z : z + 1, :] = wsum[:, z, 0:1, :]


def add_faces(wsum, face_in, plane_out):
    length_a = wsum.shape[2]
    last = slice(length_a - 1, length_a)
    for z in range(8):
        wsum[:, z, 0:1, :] = wsum[:, z, 0:1, :] + face_in[0, :, z : z + 1, :]
        wsum[:, z, last, :] = wsum[:, z, last, :] + face_in[1, :, z : z + 1, :]
    plane_out[0] = wsum[:, 7]
    plane_out[1] = wsum[:, 0]


def fluid_finish(wsum, plane_in, fluid_ref):
    for z in range(8):
        total = wsum[:, z]
        if z == 0:
            total = total + plane_in[0]
        if z == 7:
            total = total + plane_in[1]
        fluid_ref[:, z] = total[0:3] * (-1.0 / total[3:4])


def interpolate(both, const_ref, table):
    width = both.shape[1]
    point = jnp.concatenate([const_ref[ROW_POINT : ROW_POINT + 8, :]] * (width // 128), axis=1)
    norm = jnp.concatenate([const_ref[ROW_NORM : ROW_NORM + 8, :]] * (width // 128), axis=1)

    def lagrange(row):
        diff = row - point
        one = pltpu.roll(diff, 1, 0)
        two = one * pltpu.roll(one, 1, 0)
        four = two * pltpu.roll(two, 2, 0)
        rest = four * pltpu.roll(two, 4, 0) * pltpu.roll(one, 6, 0)
        return (rest * norm).astype(BF16).astype(F32)

    lag_z = lagrange(both[0:1])
    lag_a = lagrange(both[1:2])
    lag_r = lagrange(both[2:3])
    tau = both[3:4]
    element = both[4:5].astype(jnp.int32)
    radial = jnp.broadcast_to(element & 15, (8, width))
    azimuth = jnp.broadcast_to((element >> 4) & 3, (128, width))
    weight_r = jnp.concatenate(
        [jnp.where(radial == e, lag_r, 0.0) for e in range(16)], axis=0
    ).astype(BF16)
    zero = jnp.zeros_like(weight_r)
    weight = jnp.concatenate(
        [jnp.where(azimuth == e, weight_r, zero) for e in range(4)], axis=0
    )
    first = jnp.dot(table[...], weight, preferred_element_type=F32)
    sums = []
    for field in range(6):
        total = jnp.zeros((8, width), F32)
        for z in range(8):
            row = 64 * field + 8 * z
            total = total + first[row : row + 8] * lag_z[z : z + 1]
        sums.append(total * lag_a)
    return [
        jnp.sum(3.0 * sums[3 + comp] + tau * sums[comp], axis=0, keepdims=True)
        for comp in range(3)
    ]


def gather(rel8, n_xs, recvr, onehot):
    held = rel8.shape[1]
    answers = recvr[...].reshape(4 * n_xs, SLOTS)
    spread = jnp.dot(
        jnp.concatenate([p.astype(BF16) for p in split3(answers)], axis=0),
        onehot[...],
        preferred_element_type=F32,
    )
    span = 4 * n_xs
    half = lax.broadcasted_iota(jnp.int32, (8, held), 0) // 4
    total = jnp.zeros((8, held), F32)
    for pair in range(n_xs // 2):
        rows = [spread[w * span + 8 * pair : w * span + 8 * pair + 8] for w in range(3)]
        total = total + jnp.where(rel8 - half == 2 * pair, rows[0] + rows[1] + rows[2], 0.0)
    total = total + pltpu.roll(total, 4, 0)
    return total[0:3]


def kernel(
    n_ax, n_xs,
    part_ref, elem_ref, ref_ref, bvel_ref, tau_ref, coef_ref, scale_ref, const_ref, quad_ref,
    vel_hbm, hist_hbm,
    fluid_ref, bubble_ref,
    vel_ref, hist_ref, lhs, onehot, sendq, recvq, sendr, recvr, table, wsum,
    face_out, face_in, plane_out, plane_in,
    local_sem, q_send, q_recv, r_send, r_recv, h_send, h_recv,
):
    ax = lax.axis_index("ax")
    me = lax.axis_index("xs")
    held = part_ref.shape[1]
    up, down = lax.rem(ax + 1, n_ax), lax.rem(ax + n_ax - 1, n_ax)

    load_vel = pltpu.make_async_copy(vel_hbm, vel_ref, local_sem.at[0])
    load_vel.start()
    load_hist = pltpu.make_async_copy(hist_hbm, hist_ref, local_sem.at[1])
    load_hist.start()

    def wrap(place):
        return jnp.where(place >= n_xs, place - n_xs, place)

    barrier = pltpu.get_barrier_semaphore()
    for step in range(1, n_xs):
        pl.semaphore_signal(
            barrier, inc=1, device_id=(ax, wrap(me + step)), device_id_type=MESH
        )
    for other in (up, down):
        pl.semaphore_signal(barrier, inc=1, device_id=(other, me), device_id_type=MESH)

    def query_copy(first, count, group, target):
        return pltpu.make_async_remote_copy(
            src_ref=sendq.at[pl.ds(first, count), pl.ds(0, 5)],
            dst_ref=recvq.at[pl.ds(first, count), pl.ds(0, 5)],
            send_sem=q_send,
            recv_sem=q_recv.at[group],
            device_id=(ax, target),
            device_id_type=MESH,
        )

    def answer_copy(tile, count, odd, step):
        return pltpu.make_async_remote_copy(
            src_ref=sendr.at[pl.ds(tile, count), pl.ds(4 * odd, 3)],
            dst_ref=recvr.at[pl.ds(tile, count), pl.ds(4 * odd, 3)],
            send_sem=r_send.at[odd],
            recv_sem=r_recv.at[odd],
            device_id=(ax, wrap(me + n_xs - step)),
            device_id_type=MESH,
        )

    def face_copy(side):
        return pltpu.make_async_remote_copy(
            src_ref=face_out.at[side],
            dst_ref=face_in.at[side],
            send_sem=h_send.at[side],
            recv_sem=h_recv.at[side],
            device_id=(ax, wrap(me + (1 if side == 0 else n_xs - 1))),
            device_id_type=MESH,
        )

    def plane_copy(side):
        return pltpu.make_async_remote_copy(
            src_ref=plane_out.at[side],
            dst_ref=plane_in.at[side],
            send_sem=h_send.at[2 + side],
            recv_sem=h_recv.at[2 + side],
            device_id=(up if side == 0 else down, me),
            device_id_type=MESH,
        )

    rel = part_ref[...] - me
    rel = jnp.where(rel < 0, rel + n_xs, rel)
    ranked(rel, n_xs, onehot)
    coords = jnp.concatenate([ref_ref[...], tau_ref[...]], axis=0)
    dispatch(rel, n_xs, coords, elem_ref[...].astype(F32), lhs, onehot, sendq, recvq)
    pl.semaphore_wait(barrier, n_xs + 1)
    for step in range(1, n_xs):
        query_copy(step, 1, (step - 1) // GROUP, wrap(me + step)).start()

    load_vel.wait()
    advection(vel_ref, scale_ref, const_ref, table, wsum)
    azimuth_pairs(wsum, face_out)
    for side in range(2):
        face_copy(side).start()

    def serve(group, count):
        first = GROUP * group + 1
        query_copy(first, count, group, me).wait_recv()
        sources = [recvq[first + i] for i in range(count)]
        if count < GROUP:
            sources.append(recvq[0])
        values = interpolate(jnp.concatenate(sources, axis=1), const_ref, table)
        for i in range(GROUP):
            lanes = slice(SLOTS * i, SLOTS * (i + 1))
            if i == count:
                for comp in range(3):
                    recvr[0, comp : comp + 1, :] = values[comp][:, lanes]
            else:
                tile, odd = (GROUP // 2) * group + (1 + i) // 2, (1 + i) % 2
                for comp in range(3):
                    row = 4 * odd + comp
                    sendr[tile, row : row + 1, :] = values[comp][:, lanes]
                answer_copy(tile, 1, odd, first + i).start()

    groups = n_xs // GROUP

    def serve_step(group, carry):
        serve(group, GROUP)
        return carry

    lax.fori_loop(0, groups - 1, serve_step, 0)
    serve(groups - 1, GROUP - 1)

    for side in range(2):
        face_copy(side).wait()
    add_faces(wsum, face_in, plane_out)
    for side in range(2):
        plane_copy(side).start()

    load_hist.wait()
    basset = jnp.dot(quad_ref[...], hist_ref[...], preferred_element_type=F32)[0:3]
    local = coef_ref[...] * basset - tau_ref[...] * bvel_ref[...]

    for side in range(2):
        plane_copy(side).wait()
    fluid_finish(wsum, plane_in, fluid_ref)

    query_copy(1, n_xs - 1, 0, me).wait_send()
    answer_copy(1, n_xs // 2 - 1, 0, 0).wait()
    answer_copy(0, n_xs // 2, 1, 0).wait()
    rel8 = jnp.broadcast_to(rel, (8, held))
    bubble_ref[...] = gather(rel8, n_xs, recvr, onehot) + local


def shards(
    velocity, metric, bubble_part, bubble_elem, bubble_ref, bubble_vel, inv_tau,
    basset_coef, history,
):
    n_ax, n_xs = lax.axis_size("ax"), lax.axis_size("xs")
    held = bubble_part.shape[0]
    steps = history.shape[0]
    _, length_z, length_a, length_r = velocity.shape
    scale = jnp.repeat(jnp.repeat(metric[:, 0], 8, axis=1), 8, axis=2)
    const = jnp.asarray(constant_table())
    quad = jnp.asarray(quadrature_rows(steps), BF16)
    vmem = pl.BlockSpec(memory_space=pltpu.VMEM)
    anywhere = pl.BlockSpec(memory_space=pl.ANY)
    dma = pltpu.SemaphoreType.DMA
    return pl.pallas_call(
        functools.partial(kernel, n_ax, n_xs),
        out_shape=(
            jax.ShapeDtypeStruct(velocity.shape, F32),
            jax.ShapeDtypeStruct((3, held), F32),
        ),
        in_specs=[vmem] * 9 + [anywhere] * 2,
        out_specs=(vmem, vmem),
        scratch_shapes=[
            pltpu.VMEM(velocity.shape, F32),
            pltpu.VMEM((3 * steps, held), BF16),
            pltpu.VMEM((16 * n_xs, held), BF16),
            pltpu.VMEM((SLOTS, held), BF16),
            pltpu.VMEM((n_xs, 8, SLOTS), F32),
            pltpu.VMEM((n_xs, 8, SLOTS), F32),
            pltpu.VMEM((n_xs // 2, 8, SLOTS), F32),
            pltpu.VMEM((n_xs // 2, 8, SLOTS), F32),
            pltpu.VMEM((6 * 64, 4 * length_r), BF16),
            pltpu.VMEM((4, length_z, length_a, length_r), F32),
            pltpu.VMEM((2, 4, length_z, length_r), F32),
            pltpu.VMEM((2, 4, length_z, length_r), F32),
            pltpu.VMEM((2, 4, length_a, length_r), F32),
            pltpu.VMEM((2, 4, length_a, length_r), F32),
            dma((2,)),
            dma,
            dma((n_xs // GROUP,)),
            dma((2,)),
            dma((2,)),
            dma((4,)),
            dma((4,)),
        ],
        compiler_params=pltpu.CompilerParams(
            collective_id=0, has_side_effects=True, vmem_limit_bytes=40 * 1024 * 1024
        ),
    )(
        bubble_part.reshape(1, held),
        bubble_elem.reshape(1, held),
        bubble_ref,
        bubble_vel,
        inv_tau.reshape(1, held),
        basset_coef.reshape(1, held),
        scale,
        const,
        quad,
        velocity,
        history.transpose(1, 0, 2).reshape(3 * steps, held),
    )


def solution(mesh):
    return jax.shard_map(
        shards,
        mesh=mesh,
        in_specs=(
            P(None, "ax", "xs", None),
            P(None, "ax", "xs", None),
            P(("ax", "xs")),
            P(("ax", "xs")),
            P(None, ("ax", "xs")),
            P(None, ("ax", "xs")),
            P(("ax", "xs")),
            P(("ax", "xs")),
            P(None, None, ("ax", "xs")),
        ),
        out_specs=(P(None, "ax", "xs", None), P(None, ("ax", "xs"))),
        check_vma=False,
    )
```

```python
import functools

import jax
import jax.numpy as jnp
import numpy as np
from jax import lax
from jax.experimental import pallas as pl
from jax.experimental.pallas import tpu as pltpu
from jax.sharding import PartitionSpec as P

GLL_POINTS = (
    -1.0,
    -0.8717401485096066,
    -0.5917001814331423,
    -0.2092992179024789,
    0.2092992179024789,
    0.5917001814331423,
    0.8717401485096066,
    1.0,
)
GLL_WEIGHTS = (
    0.03571428571428571,
    0.21070422714350603,
    0.34112269248350435,
    0.4124587946587039,
    0.4124587946587039,
    0.34112269248350435,
    0.21070422714350603,
    0.03571428571428571,
)
SLOTS = 128
GROUP = 4
MESH = pl.DeviceIdType.MESH
F32 = jnp.float32
BF16 = jnp.bfloat16


def derivative_matrix():
    points = np.array(GLL_POINTS)
    identity = np.eye(8)
    spread = points[:, None] - points[None, :] + identity
    products = np.prod(spread, axis=1)
    matrix = products[:, None] / products[None, :] / spread
    off_diagonal = matrix * (1.0 - identity)
    return off_diagonal - identity * off_diagonal.sum(axis=1)[:, None]


DMAT = derivative_matrix()

ROW_POINT = 0
ROW_NORM = 8
ROW_ROLL = 16
ROW_WEIGHT = 80
ROW_RADIAL = 112
ROW_QUAD = 240


def constant_table(steps):
    points = np.array(GLL_POINTS)
    weights = np.array(GLL_WEIGHTS)
    rows = [np.repeat(points[:, None], 128, axis=1)]
    spread = points[:, None] - points[None, :] + np.eye(8)
    rows.append(np.repeat((1.0 / np.prod(spread, axis=1))[:, None], 128, axis=1))
    for shift in range(8):
        coef = np.array([DMAT[i, (i - shift) % 8] for i in range(8)])
        rows.append(np.repeat(coef[:, None], 128, axis=1))
    rows.append(np.tile(weights, 4)[:, None] * np.tile(weights, 16)[None, :])
    rows.append(np.kron(np.eye(16), DMAT.T))
    rows += quadrature_rows(steps)
    return np.concatenate(rows, axis=0).astype(np.float32)


def quadrature_rows(length):
    steps = np.arange(length, dtype=np.float32)
    quad = np.sqrt(steps + np.float32(1.0)) - np.sqrt(steps)
    rows = np.zeros((3, 8, length), np.float32)
    for comp in range(3):
        rows[comp, comp] = quad
    return list(rows)


def peers_by_distance(n_xs):
    length_x, length_y, cores = {32: (4, 4, 2), 4: (2, 1, 2)}[n_xs]
    offsets = [
        (dx, dy, core)
        for dx in range(length_x)
        for dy in range(length_y)
        for core in range(cores)
    ]

    def distance(offset):
        return min(offset[0], length_x - offset[0]) + min(offset[1], length_y - offset[1])

    return (length_x, length_y, cores), sorted(offsets, key=distance)


def split3(values):
    high = values.astype(BF16).astype(F32)
    rest = values - high
    mid = rest.astype(BF16).astype(F32)
    return high, mid, rest - mid


def ranked(rel, n_xs, onehot):
    held = rel.shape[1]
    member = (
        jnp.broadcast_to(rel, (n_xs, held))
        == lax.broadcasted_iota(jnp.int32, (n_xs, held), 0)
    ).astype(F32)
    chunks = held // 128
    pieces = [member[:, c * 128 : (c + 1) * 128] for c in range(chunks)]
    stacked = jnp.concatenate(pieces, axis=0).astype(BF16)
    before = (
        lax.broadcasted_iota(jnp.int32, (128, 128), 0)
        < lax.broadcasted_iota(jnp.int32, (128, 128), 1)
    ).astype(F32).astype(BF16)
    counts = jnp.dot(stacked, before, preferred_element_type=F32)
    totals = jnp.dot(stacked, jnp.ones((128, 128), BF16), preferred_element_type=F32)
    carry = jnp.zeros((n_xs, 128), F32)
    ranks = []
    for c in range(chunks):
        rows = slice(c * n_xs, (c + 1) * n_xs)
        ranks.append(jnp.sum(pieces[c] * (counts[rows] + carry), axis=0, keepdims=True))
        carry = carry + totals[rows]
    rank = jnp.concatenate(ranks, axis=1).astype(jnp.int32)
    onehot[...] = (
        jnp.broadcast_to(rank, (SLOTS, held))
        == lax.broadcasted_iota(jnp.int32, (SLOTS, held), 0)
    ).astype(F32).astype(BF16)


def dispatch(rel, codes, coords, elem, lhs, onehot, sendq, recvq):
    held = rel.shape[1]
    high, mid, low = split3(coords)
    packed = jnp.concatenate(
        [high, elem, jnp.zeros((3, held), F32), mid, low], axis=0
    ).astype(BF16)
    rel16 = jnp.broadcast_to(rel, (16, held))
    zero = jnp.zeros((16, held), BF16)
    n_xs = len(codes)
    for place, code in enumerate(codes):
        lhs[16 * place : 16 * place + 16, :] = jnp.where(rel16 == code, packed, zero)
    slots = lax.dot_general(
        lhs[...], onehot[...], (((1,), (1,)), ((), ())), preferred_element_type=F32
    ).reshape(n_xs, 2, 8, SLOTS)
    rest = slots[:, 1]
    rest = rest + pltpu.roll(rest, 4, 1)
    row = lax.broadcasted_iota(jnp.int32, (n_xs, 8, SLOTS), 1)
    slots = slots[:, 0] + jnp.where(row < 4, rest, 0.0)
    sendq[...] = slots
    recvq[0] = slots[0]


def advection(vel_ref, metric_ref, const_ref, table, wsum):
    vel = vel_ref[...]
    length_a, length_r = vel.shape[2], vel.shape[3]
    nodes = 8 * length_a
    grad_r = jnp.dot(
        vel.reshape(3 * nodes, length_r),
        const_ref[ROW_RADIAL : ROW_RADIAL + 128, :],
        preferred_element_type=F32,
        precision=lax.Precision.HIGHEST,
    ).reshape(vel.shape)
    spread = (
        lax.broadcasted_iota(jnp.int32, (length_r // 8, length_r), 1) // 8
        == lax.broadcasted_iota(jnp.int32, (length_r // 8, length_r), 0)
    ).astype(F32)
    scale = []
    for factor in range(3):
        rows = jnp.dot(
            metric_ref[factor], spread, preferred_element_type=F32, precision=lax.Precision.HIGHEST
        )
        scale.append(
            jnp.concatenate(
                [
                    jnp.broadcast_to(rows[e : e + 1], (8, length_r))
                    for e in range(length_a // 8)
                ],
                axis=0,
            )
        )
    inverse = const_ref[ROW_WEIGHT : ROW_WEIGHT + 32, :] / (scale[0] * scale[1] * scale[2])
    lane = lax.broadcasted_iota(jnp.int32, (4, length_a, length_r), 2)
    upper = (lane % 8 == 7) & (lane < length_r - 1)
    lower = (lane % 8 == 0) & (lane > 0)
    for z in range(8):
        here = vel[:, z]
        grad_z = sum(float(DMAT[z, j]) * vel[:, j] for j in range(8) if abs(DMAT[z, j]) > 1e-9)
        groups = here.reshape(3 * length_a // 8, 8, length_r)
        grad_a = const_ref[ROW_ROLL : ROW_ROLL + 8, :] * groups
        for shift in range(1, 8):
            coef = const_ref[ROW_ROLL + 8 * shift : ROW_ROLL + 8 * shift + 8, :]
            grad_a = grad_a + coef * pltpu.roll(groups, shift, 1)
        grad_a = grad_a.reshape(here.shape)
        advect = (
            (here[0] * scale[0])[None] * grad_z
            + (here[1] * scale[1])[None] * grad_a
            + (here[2] * scale[2])[None] * grad_r[:, z]
        )
        fields = [here[0], here[1], here[2], advect[0], advect[1], advect[2]]
        if z % 2 == 1:
            for field in range(6):
                for element in range(length_a // 8):
                    rows = slice(8 * element, 8 * element + 8)
                    pair = jnp.concatenate([earlier[field][rows], fields[field][rows]], axis=0)
                    table[
                        64 * field + 8 * (z - 1) : 64 * field + 8 * (z + 1),
                        length_r * element : length_r * (element + 1),
                    ] = pair.astype(BF16)
        earlier = fields
        mass = GLL_WEIGHTS[z] * inverse
        weighted = jnp.concatenate([mass[None] * advect, mass[None]], axis=0)
        after = pltpu.roll(weighted, length_r - 1, 2)
        prior = pltpu.roll(weighted, 1, 2)
        wsum[:, z] = weighted + jnp.where(upper, after, jnp.where(lower, prior, 0.0))


def azimuth_pairs(wsum, face_out):
    length_a = wsum.shape[2]
    for edge in range(8, length_a, 8):
        both = wsum[:, :, edge - 1 : edge, :] + wsum[:, :, edge : edge + 1, :]
        wsum[:, :, edge - 1 : edge, :] = both
        wsum[:, :, edge : edge + 1, :] = both
    for z in range(8):
        face_out[0, :, z : z + 1, :] = wsum[:, z, length_a - 1 : length_a, :]
        face_out[1, :, z : z + 1, :] = wsum[:, z, 0:1, :]


def add_faces(wsum, face_in, plane_out):
    length_a = wsum.shape[2]
    last = slice(length_a - 1, length_a)
    for z in range(8):
        wsum[:, z, 0:1, :] = wsum[:, z, 0:1, :] + face_in[0, :, z : z + 1, :]
        wsum[:, z, last, :] = wsum[:, z, last, :] + face_in[1, :, z : z + 1, :]
    plane_out[0] = wsum[:, 7]
    plane_out[1] = wsum[:, 0]


def fluid_finish(wsum, plane_in, fluid_ref):
    for z in range(8):
        total = wsum[:, z]
        if z == 0:
            total = total + plane_in[0]
        if z == 7:
            total = total + plane_in[1]
        fluid_ref[:, z] = total[0:3] * (-1.0 / total[3:4])


def interpolate(both, const_ref, table):
    width = both.shape[1]
    point = jnp.concatenate([const_ref[ROW_POINT : ROW_POINT + 8, :]] * (width // 128), axis=1)
    norm = jnp.concatenate([const_ref[ROW_NORM : ROW_NORM + 8, :]] * (width // 128), axis=1)

    def lagrange(row):
        diff = row - point
        one = pltpu.roll(diff, 1, 0)
        two = one * pltpu.roll(one, 1, 0)
        four = two * pltpu.roll(two, 2, 0)
        rest = four * pltpu.roll(two, 4, 0) * pltpu.roll(one, 6, 0)
        return (rest * norm).astype(BF16).astype(F32)

    lag_z = lagrange(both[0:1])
    lag_a = lagrange(both[1:2])
    lag_r = lagrange(both[2:3])
    tau = both[3:4]
    element = both[4:5].astype(jnp.int32)
    radial = jnp.broadcast_to(element & 15, (8, width))
    azimuth = jnp.broadcast_to((element >> 4) & 3, (128, width))
    weight_r = jnp.concatenate(
        [jnp.where(radial == e, lag_r, 0.0) for e in range(16)], axis=0
    ).astype(BF16)
    zero = jnp.zeros_like(weight_r)
    weight = jnp.concatenate(
        [jnp.where(azimuth == e, weight_r, zero) for e in range(4)], axis=0
    )
    first = jnp.dot(table[...], weight, preferred_element_type=F32)
    sums = []
    for field in range(6):
        total = jnp.zeros((8, width), F32)
        for z in range(8):
            row = 64 * field + 8 * z
            total = total + first[row : row + 8] * lag_z[z : z + 1]
        sums.append(total * lag_a)
    return [
        jnp.sum(3.0 * sums[3 + comp] + tau * sums[comp], axis=0, keepdims=True)
        for comp in range(3)
    ]


def gather(rel, codes, recvr, onehot):
    held = rel.shape[1]
    n_xs = len(codes)
    rel8 = jnp.broadcast_to(rel, (8, held))
    answers = recvr[...].reshape(4 * n_xs, SLOTS)
    spread = jnp.dot(
        jnp.concatenate([p.astype(BF16) for p in split3(answers)], axis=0),
        onehot[...],
        preferred_element_type=F32,
    )
    span = 4 * n_xs
    half = lax.broadcasted_iota(jnp.int32, (8, held), 0) < 4
    total = jnp.zeros((8, held), F32)
    for pair in range(n_xs // 2):
        rows = [spread[w * span + 8 * pair : w * span + 8 * pair + 8] for w in range(3)]
        code = jnp.where(half, codes[2 * pair], codes[2 * pair + 1])
        total = total + jnp.where(rel8 == code, rows[0] + rows[1] + rows[2], 0.0)
    total = total + pltpu.roll(total, 4, 0)
    return total[0:3]


def kernel(
    n_ax, n_xs,
    part_hbm, elem_hbm, ref_hbm, tau_hbm, vel_hbm, metric_hbm, const_hbm, bvel_hbm, coef_hbm,
    hist_hbm,
    fluid_hbm, bubble_ref,
    part_ref, elem_ref, ref_ref, tau_ref, vel_ref, metric_ref, const_ref, bvel_ref, coef_ref,
    hist_ref,
    fluid_ref, lhs, onehot, sendq, recvq, sendr, recvr, table, wsum, face_out, face_in, plane_out, plane_in,
    local_sem, q_send, q_recv, r_send, r_recv, h_send, h_recv,
):
    ax = lax.axis_index("ax")
    me = lax.axis_index("xs")
    held = part_ref.shape[1]
    (length_x, length_y, cores), offsets = peers_by_distance(n_xs)
    codes = [(dx * length_y + dy) * cores + core for dx, dy, core in offsets]

    loads = [
        pltpu.make_async_copy(source, target, local_sem.at[i])
        for i, (source, target) in enumerate(
            [
                (part_hbm, part_ref), (elem_hbm, elem_ref), (ref_hbm, ref_ref),
                (tau_hbm, tau_ref), (vel_hbm, vel_ref), (metric_hbm, metric_ref),
                (const_hbm, const_ref), (bvel_hbm, bvel_ref), (coef_hbm, coef_ref),
                (hist_hbm, hist_ref),
            ]
        )
    ]
    for load in loads:
        load.start()

    def wrap(place, length):
        return jnp.where(place >= length, place - length, place)

    here_x = lax.div(me, length_y * cores)
    here_y = lax.rem(lax.div(me, cores), length_y)
    here_core = lax.rem(me, cores)
    places_x = [wrap(here_x + d, length_x) * (length_y * cores) for d in range(length_x)]
    places_y = [wrap(here_y + d, length_y) * cores for d in range(length_y)]
    places_core = [wrap(here_core + d, cores) for d in range(cores)]

    def ahead(place):
        dx, dy, core = offsets[place]
        return places_x[dx] + places_y[dy] + places_core[core]

    def behind(place):
        dx, dy, core = offsets[place]
        return (
            places_x[(length_x - dx) % length_x]
            + places_y[(length_y - dy) % length_y]
            + places_core[(cores - core) % cores]
        )

    up, down = wrap(ax + 1, n_ax), wrap(ax + n_ax - 1, n_ax)
    left, right = wrap(me + n_xs - 1, n_xs), wrap(me + 1, n_xs)

    barrier = pltpu.get_barrier_semaphore()
    for place in range(n_xs - 1, 0, -1):
        pl.semaphore_signal(barrier, inc=1, device_id=(ax, behind(place)), device_id_type=MESH)
    for other in (up, down):
        pl.semaphore_signal(barrier, inc=1, device_id=(other, me), device_id_type=MESH)

    def query_copy(first, count, group, target):
        return pltpu.make_async_remote_copy(
            src_ref=sendq.at[pl.ds(first, count), pl.ds(0, 5)],
            dst_ref=recvq.at[pl.ds(first, count), pl.ds(0, 5)],
            send_sem=q_send,
            recv_sem=q_recv.at[group],
            device_id=(ax, target),
            device_id_type=MESH,
        )

    def answer_copy(tile, count, odd, target):
        return pltpu.make_async_remote_copy(
            src_ref=sendr.at[pl.ds(tile, count), pl.ds(4 * odd, 3)],
            dst_ref=recvr.at[pl.ds(tile, count), pl.ds(4 * odd, 3)],
            send_sem=r_send.at[odd],
            recv_sem=r_recv.at[odd],
            device_id=(ax, target),
            device_id_type=MESH,
        )

    def face_copy(side):
        return pltpu.make_async_remote_copy(
            src_ref=face_out.at[side],
            dst_ref=face_in.at[side],
            send_sem=h_send.at[side],
            recv_sem=h_recv.at[side],
            device_id=(ax, right if side == 0 else left),
            device_id_type=MESH,
        )

    def plane_copy(side):
        return pltpu.make_async_remote_copy(
            src_ref=plane_out.at[side],
            dst_ref=plane_in.at[side],
            send_sem=h_send.at[2 + side],
            recv_sem=h_recv.at[2 + side],
            device_id=(up if side == 0 else down, me),
            device_id_type=MESH,
        )

    for load in loads[0:4]:
        load.wait()
    part = part_ref[...]
    far_x = part // (length_y * cores) - here_x
    far_y = (part // cores) % length_y - here_y
    far_core = part % cores - here_core
    rel = (
        jnp.where(far_x < 0, far_x + length_x, far_x) * (length_y * cores)
        + jnp.where(far_y < 0, far_y + length_y, far_y) * cores
        + jnp.where(far_core < 0, far_core + cores, far_core)
    )
    ranked(rel, n_xs, onehot)
    coords = jnp.concatenate([ref_ref[...], tau_ref[...]], axis=0)
    dispatch(rel, codes, coords, elem_ref[...].astype(F32), lhs, onehot, sendq, recvq)
    for load in loads[4:7]:
        load.wait()
    advection(vel_ref, metric_ref, const_ref, table, wsum)
    azimuth_pairs(wsum, face_out)
    pl.semaphore_wait(barrier, n_xs + 1)
    for side in range(2):
        face_copy(side).start()
    for place in range(n_xs - 1, 0, -1):
        query_copy(place, 1, place // GROUP, ahead(place)).start()

    groups = n_xs // GROUP
    for group in range(groups):
        if group == min(3, groups - 1):
            for side in range(2):
                face_copy(side).wait()
            add_faces(wsum, face_in, plane_out)
            for side in range(2):
                plane_copy(side).start()
        first = GROUP * group
        skip = 1 if group == 0 else 0
        query_copy(first + skip, GROUP - skip, group, me).wait_recv()
        sources = [recvq[first + i] for i in range(GROUP)]
        values = interpolate(jnp.concatenate(sources, axis=1), const_ref, table)
        for i in range(GROUP):
            place = first + i
            lanes = slice(SLOTS * i, SLOTS * (i + 1))
            target = sendr if place > 0 else recvr
            for comp in range(3):
                row = 4 * (place % 2) + comp
                target[place // 2, row : row + 1, :] = values[comp][:, lanes]
            if place > 0:
                answer_copy(place // 2, 1, place % 2, behind(place)).start()

    for load in loads[7:]:
        load.wait()
    quad = jnp.concatenate(
        [const_ref[ROW_QUAD + 8 * comp : ROW_QUAD + 8 * comp + 8, :] for comp in range(3)], axis=1
    )
    quad = jnp.concatenate([quad, jnp.zeros_like(quad)], axis=0).astype(BF16)
    basset = jnp.dot(quad, hist_ref[...], preferred_element_type=F32)[0:3]
    local = coef_ref[...] * basset - tau_ref[...] * bvel_ref[...]

    for side in range(2):
        plane_copy(side).wait()
    fluid_finish(wsum, plane_in, fluid_ref)
    store_fluid = pltpu.make_async_copy(fluid_ref, fluid_hbm, local_sem.at[len(loads)])
    store_fluid.start()

    query_copy(1, n_xs - 1, 0, me).wait_send()
    answer_copy(1, n_xs // 2 - 1, 0, me).wait()
    answer_copy(0, n_xs // 2, 1, me).wait()
    bubble_ref[...] = gather(rel, codes, recvr, onehot) + local
    store_fluid.wait()


def store(fluid_in, bubble_in, fluid_out, bubble_out, fluid_ref, bubble_ref, in_sems, out_sems):
    pieces = [(fluid_in.at[c], fluid_ref.at[c], fluid_out.at[c]) for c in range(3)]
    pieces.append((bubble_in, bubble_ref, bubble_out))
    reads = [pltpu.make_async_copy(p[0], p[1], in_sems.at[i]) for i, p in enumerate(pieces)]
    writes = [pltpu.make_async_copy(p[1], p[2], out_sems.at[i]) for i, p in enumerate(pieces)]
    for read in reads:
        read.start()
    for read, write in zip(reads, writes):
        read.wait()
        write.start()
    for write in writes:
        write.wait()


def shards(
    velocity, metric, bubble_part, bubble_elem, bubble_ref, bubble_vel, inv_tau,
    basset_coef, history,
):
    n_ax, n_xs = lax.axis_size("ax"), lax.axis_size("xs")
    held = bubble_part.shape[0]
    steps = history.shape[0]
    _, length_z, length_a, length_r = velocity.shape
    vmem = pl.BlockSpec(memory_space=pltpu.VMEM)
    anywhere = pl.BlockSpec(memory_space=pl.ANY)
    dma = pltpu.SemaphoreType.DMA
    outputs = (
        jax.ShapeDtypeStruct(velocity.shape, F32),
        jax.ShapeDtypeStruct((3, held), F32),
    )
    operands = [
        bubble_part.reshape(1, held),
        bubble_elem.reshape(1, held),
        bubble_ref,
        inv_tau.reshape(1, held),
        velocity,
        metric.reshape(3, length_a // 8, length_r // 8),
        jnp.asarray(constant_table(steps)),
        bubble_vel,
        basset_coef.reshape(1, held),
        history.transpose(1, 0, 2).reshape(3 * steps, held),
    ]
    results = pl.pallas_call(
        functools.partial(kernel, n_ax, n_xs),
        out_shape=outputs,
        in_specs=[anywhere] * len(operands),
        out_specs=(anywhere, vmem),
        scratch_shapes=[pltpu.VMEM(o.shape, o.dtype) for o in operands]
        + [
            pltpu.VMEM(velocity.shape, F32),
            pltpu.VMEM((16 * n_xs, held), BF16),
            pltpu.VMEM((SLOTS, held), BF16),
            pltpu.VMEM((n_xs, 8, SLOTS), F32),
            pltpu.VMEM((n_xs, 8, SLOTS), F32),
            pltpu.VMEM((n_xs // 2, 8, SLOTS), F32),
            pltpu.VMEM((n_xs // 2, 8, SLOTS), F32),
            pltpu.VMEM((6 * 64, 4 * length_r), BF16),
            pltpu.VMEM((4, length_z, length_a, length_r), F32),
            pltpu.VMEM((2, 4, length_z, length_r), F32),
            pltpu.VMEM((2, 4, length_z, length_r), F32),
            pltpu.VMEM((2, 4, length_a, length_r), F32),
            pltpu.VMEM((2, 4, length_a, length_r), F32),
            dma((len(operands) + 1,)),
            dma,
            dma((n_xs // GROUP,)),
            dma((2,)),
            dma((2,)),
            dma((4,)),
            dma((4,)),
        ],
        compiler_params=pltpu.CompilerParams(
            collective_id=0, has_side_effects=True, vmem_limit_bytes=56 * 1024 * 1024
        ),
    )(*operands)
    return pl.pallas_call(
        store,
        out_shape=outputs,
        in_specs=[anywhere, anywhere],
        out_specs=(anywhere, anywhere),
        scratch_shapes=[pltpu.VMEM(o.shape, o.dtype) for o in outputs] + [dma((4,)), dma((4,))],
        compiler_params=pltpu.CompilerParams(vmem_limit_bytes=56 * 1024 * 1024),
    )(*results)


def solution(mesh):
    return jax.shard_map(
        shards,
        mesh=mesh,
        in_specs=(
            P(None, "ax", "xs", None),
            P(None, "ax", "xs", None),
            P(("ax", "xs")),
            P(("ax", "xs")),
            P(None, ("ax", "xs")),
            P(None, ("ax", "xs")),
            P(("ax", "xs")),
            P(("ax", "xs")),
            P(None, None, ("ax", "xs")),
        ),
        out_specs=(P(None, "ax", "xs", None), P(None, ("ax", "xs"))),
        check_vma=False,
    )
```

```python
import functools

import jax
import jax.numpy as jnp
import numpy as np
from jax import lax
from jax.experimental import pallas as pl
from jax.experimental.pallas import tpu as pltpu
from jax.sharding import PartitionSpec as P

GLL_POINTS = (
    -1.0,
    -0.8717401485096066,
    -0.5917001814331423,
    -0.2092992179024789,
    0.2092992179024789,
    0.5917001814331423,
    0.8717401485096066,
    1.0,
)
GLL_WEIGHTS = (
    0.03571428571428571,
    0.21070422714350603,
    0.34112269248350435,
    0.4124587946587039,
    0.4124587946587039,
    0.34112269248350435,
    0.21070422714350603,
    0.03571428571428571,
)
SLOTS = 128
GROUP = 4
MESH = pl.DeviceIdType.MESH
F32 = jnp.float32
BF16 = jnp.bfloat16


def derivative_matrix():
    points = np.array(GLL_POINTS)
    identity = np.eye(8)
    spread = points[:, None] - points[None, :] + identity
    products = np.prod(spread, axis=1)
    matrix = products[:, None] / products[None, :] / spread
    off_diagonal = matrix * (1.0 - identity)
    return off_diagonal - identity * off_diagonal.sum(axis=1)[:, None]


DMAT = derivative_matrix()

ROW_POINT = 0
ROW_NORM = 8
ROW_ROLL = 16
ROW_WEIGHT = 80
ROW_RADIAL = 112
ROW_QUAD = 240


def constant_table(steps):
    points = np.array(GLL_POINTS)
    weights = np.array(GLL_WEIGHTS)
    rows = [np.repeat(points[:, None], 128, axis=1)]
    spread = points[:, None] - points[None, :] + np.eye(8)
    rows.append(np.repeat((1.0 / np.prod(spread, axis=1))[:, None], 128, axis=1))
    for shift in range(8):
        coef = np.array([DMAT[i, (i - shift) % 8] for i in range(8)])
        rows.append(np.repeat(coef[:, None], 128, axis=1))
    rows.append(np.tile(weights, 4)[:, None] * np.tile(weights, 16)[None, :])
    rows.append(np.kron(np.eye(16), DMAT.T))
    rows += quadrature_rows(steps)
    return np.concatenate(rows, axis=0).astype(np.float32)


def quadrature_rows(length):
    steps = np.arange(length, dtype=np.float32)
    quad = np.sqrt(steps + np.float32(1.0)) - np.sqrt(steps)
    rows = np.zeros((3, 8, length), np.float32)
    for comp in range(3):
        rows[comp, comp] = quad
    return list(rows)


def peers_by_distance(n_xs):
    length_x, length_y, cores = {32: (4, 4, 2), 4: (2, 1, 2)}[n_xs]
    offsets = [
        (dx, dy, core)
        for dx in range(length_x)
        for dy in range(length_y)
        for core in range(cores)
    ]

    def distance(offset):
        return min(offset[0], length_x - offset[0]) + min(offset[1], length_y - offset[1])

    return (length_x, length_y, cores), sorted(offsets, key=distance)


def split3(values):
    high = values.astype(BF16).astype(F32)
    rest = values - high
    mid = rest.astype(BF16).astype(F32)
    return high, mid, rest - mid


def ranked(rel, n_xs, onehot):
    held = rel.shape[1]
    member = (
        jnp.broadcast_to(rel, (n_xs, held))
        == lax.broadcasted_iota(jnp.int32, (n_xs, held), 0)
    ).astype(F32)
    chunks = held // 128
    pieces = [member[:, c * 128 : (c + 1) * 128] for c in range(chunks)]
    stacked = jnp.concatenate(pieces, axis=0).astype(BF16)
    before = (
        lax.broadcasted_iota(jnp.int32, (128, 128), 0)
        < lax.broadcasted_iota(jnp.int32, (128, 128), 1)
    ).astype(F32).astype(BF16)
    counts = jnp.dot(stacked, before, preferred_element_type=F32)
    totals = jnp.dot(stacked, jnp.ones((128, 128), BF16), preferred_element_type=F32)
    carry = jnp.zeros((n_xs, 128), F32)
    ranks = []
    for c in range(chunks):
        rows = slice(c * n_xs, (c + 1) * n_xs)
        ranks.append(jnp.sum(pieces[c] * (counts[rows] + carry), axis=0, keepdims=True))
        carry = carry + totals[rows]
    rank = jnp.concatenate(ranks, axis=1).astype(jnp.int32)
    onehot[...] = (
        jnp.broadcast_to(rank, (SLOTS, held))
        == lax.broadcasted_iota(jnp.int32, (SLOTS, held), 0)
    ).astype(F32).astype(BF16)


def dispatch(rel, codes, coords, elem, lhs, onehot, sendq, recvq):
    held = rel.shape[1]
    high, mid, low = split3(coords)
    packed = jnp.concatenate(
        [high, elem, jnp.zeros((3, held), F32), mid, low], axis=0
    ).astype(BF16)
    rel16 = jnp.broadcast_to(rel, (16, held))
    zero = jnp.zeros((16, held), BF16)
    n_xs = len(codes)
    for place, code in enumerate(codes):
        lhs[16 * place : 16 * place + 16, :] = jnp.where(rel16 == code, packed, zero)
    slots = lax.dot_general(
        lhs[...], onehot[...], (((1,), (1,)), ((), ())), preferred_element_type=F32
    ).reshape(n_xs, 2, 8, SLOTS)
    rest = slots[:, 1]
    rest = rest + pltpu.roll(rest, 4, 1)
    row = lax.broadcasted_iota(jnp.int32, (n_xs, 8, SLOTS), 1)
    slots = slots[:, 0] + jnp.where(row < 4, rest, 0.0)
    sendq[...] = slots
    recvq[0] = slots[0]


def advection(vel_ref, metric_ref, const_ref, table, wsum):
    vel = vel_ref[...]
    length_a, length_r = vel.shape[2], vel.shape[3]
    nodes = 8 * length_a
    grad_r = jnp.dot(
        vel.reshape(3 * nodes, length_r),
        const_ref[ROW_RADIAL : ROW_RADIAL + 128, :],
        preferred_element_type=F32,
        precision=lax.Precision.HIGHEST,
    ).reshape(vel.shape)
    spread = (
        lax.broadcasted_iota(jnp.int32, (length_r // 8, length_r), 1) // 8
        == lax.broadcasted_iota(jnp.int32, (length_r // 8, length_r), 0)
    ).astype(F32)
    scale = []
    for factor in range(3):
        rows = jnp.dot(
            metric_ref[factor], spread, preferred_element_type=F32, precision=lax.Precision.HIGHEST
        )
        scale.append(
            jnp.concatenate(
                [
                    jnp.broadcast_to(rows[e : e + 1], (8, length_r))
                    for e in range(length_a // 8)
                ],
                axis=0,
            )
        )
    inverse = const_ref[ROW_WEIGHT : ROW_WEIGHT + 32, :] / (scale[0] * scale[1] * scale[2])
    lane = lax.broadcasted_iota(jnp.int32, (4, length_a, length_r), 2)
    upper = (lane % 8 == 7) & (lane < length_r - 1)
    lower = (lane % 8 == 0) & (lane > 0)
    for z in range(8):
        here = vel[:, z]
        grad_z = sum(float(DMAT[z, j]) * vel[:, j] for j in range(8) if abs(DMAT[z, j]) > 1e-9)
        groups = here.reshape(3 * length_a // 8, 8, length_r)
        grad_a = const_ref[ROW_ROLL : ROW_ROLL + 8, :] * groups
        for shift in range(1, 8):
            coef = const_ref[ROW_ROLL + 8 * shift : ROW_ROLL + 8 * shift + 8, :]
            grad_a = grad_a + coef * pltpu.roll(groups, shift, 1)
        grad_a = grad_a.reshape(here.shape)
        advect = (
            (here[0] * scale[0])[None] * grad_z
            + (here[1] * scale[1])[None] * grad_a
            + (here[2] * scale[2])[None] * grad_r[:, z]
        )
        fields = [here[0], here[1], here[2], advect[0], advect[1], advect[2]]
        if z % 2 == 1:
            for field in range(6):
                for element in range(length_a // 8):
                    rows = slice(8 * element, 8 * element + 8)
                    pair = jnp.concatenate([earlier[field][rows], fields[field][rows]], axis=0)
                    table[
                        64 * field + 8 * (z - 1) : 64 * field + 8 * (z + 1),
                        length_r * element : length_r * (element + 1),
                    ] = pair.astype(BF16)
        earlier = fields
        mass = GLL_WEIGHTS[z] * inverse
        weighted = jnp.concatenate([mass[None] * advect, mass[None]], axis=0)
        after = pltpu.roll(weighted, length_r - 1, 2)
        prior = pltpu.roll(weighted, 1, 2)
        wsum[:, z] = weighted + jnp.where(upper, after, jnp.where(lower, prior, 0.0))


def azimuth_pairs(wsum, face_out):
    length_a = wsum.shape[2]
    for edge in range(8, length_a, 8):
        both = wsum[:, :, edge - 1 : edge, :] + wsum[:, :, edge : edge + 1, :]
        wsum[:, :, edge - 1 : edge, :] = both
        wsum[:, :, edge : edge + 1, :] = both
    for z in range(8):
        face_out[0, :, z : z + 1, :] = wsum[:, z, length_a - 1 : length_a, :]
        face_out[1, :, z : z + 1, :] = wsum[:, z, 0:1, :]


def add_faces(wsum, face_in, plane_out):
    length_a = wsum.shape[2]
    last = slice(length_a - 1, length_a)
    for z in range(8):
        wsum[:, z, 0:1, :] = wsum[:, z, 0:1, :] + face_in[0, :, z : z + 1, :]
        wsum[:, z, last, :] = wsum[:, z, last, :] + face_in[1, :, z : z + 1, :]
    plane_out[0] = wsum[:, 7]
    plane_out[1] = wsum[:, 0]


def fluid_finish(wsum, plane_in, fluid_ref):
    for z in range(8):
        total = wsum[:, z]
        if z == 0:
            total = total + plane_in[0]
        if z == 7:
            total = total + plane_in[1]
        fluid_ref[:, z] = total[0:3] * (-1.0 / total[3:4])


def interpolate(both, const_ref, table):
    width = both.shape[1]
    point = jnp.concatenate([const_ref[ROW_POINT : ROW_POINT + 8, :]] * (width // 128), axis=1)
    norm = jnp.concatenate([const_ref[ROW_NORM : ROW_NORM + 8, :]] * (width // 128), axis=1)

    def lagrange(row):
        diff = row - point
        one = pltpu.roll(diff, 1, 0)
        two = one * pltpu.roll(one, 1, 0)
        four = two * pltpu.roll(two, 2, 0)
        rest = four * pltpu.roll(two, 4, 0) * pltpu.roll(one, 6, 0)
        return (rest * norm).astype(BF16).astype(F32)

    lag_z = lagrange(both[0:1])
    lag_a = lagrange(both[1:2])
    lag_r = lagrange(both[2:3])
    tau = both[3:4]
    element = both[4:5].astype(jnp.int32)
    radial = jnp.broadcast_to(element & 15, (8, width))
    azimuth = jnp.broadcast_to((element >> 4) & 3, (128, width))
    weight_r = jnp.concatenate(
        [jnp.where(radial == e, lag_r, 0.0) for e in range(16)], axis=0
    ).astype(BF16)
    zero = jnp.zeros_like(weight_r)
    weight = jnp.concatenate(
        [jnp.where(azimuth == e, weight_r, zero) for e in range(4)], axis=0
    )
    first = jnp.dot(table[...], weight, preferred_element_type=F32)
    sums = []
    for field in range(6):
        total = jnp.zeros((8, width), F32)
        for z in range(8):
            row = 64 * field + 8 * z
            total = total + first[row : row + 8] * lag_z[z : z + 1]
        sums.append(total * lag_a)
    return [
        jnp.sum(3.0 * sums[3 + comp] + tau * sums[comp], axis=0, keepdims=True)
        for comp in range(3)
    ]


def gather(rel, codes, recvr, onehot):
    held = rel.shape[1]
    n_xs = len(codes)
    rel8 = jnp.broadcast_to(rel, (8, held))
    answers = recvr[...].reshape(4 * n_xs, SLOTS)
    spread = jnp.dot(
        jnp.concatenate([p.astype(BF16) for p in split3(answers)], axis=0),
        onehot[...],
        preferred_element_type=F32,
    )
    span = 4 * n_xs
    half = lax.broadcasted_iota(jnp.int32, (8, held), 0) < 4
    total = jnp.zeros((8, held), F32)
    for pair in range(n_xs // 2):
        rows = [spread[w * span + 8 * pair : w * span + 8 * pair + 8] for w in range(3)]
        code = jnp.where(half, codes[2 * pair], codes[2 * pair + 1])
        total = total + jnp.where(rel8 == code, rows[0] + rows[1] + rows[2], 0.0)
    total = total + pltpu.roll(total, 4, 0)
    return total[0:3]


def kernel(
    n_ax, n_xs,
    part_hbm, elem_hbm, ref_hbm, tau_hbm, vel_hbm, metric_hbm, const_hbm, bvel_hbm, coef_hbm,
    hist_hbm,
    fluid_hbm, bubble_ref,
    part_ref, elem_ref, ref_ref, tau_ref, vel_ref, metric_ref, const_ref, bvel_ref, coef_ref,
    hist_ref,
    fluid_ref, lhs, onehot, sendq, recvq, sendr, recvr, table, wsum, face_out, face_in, plane_out, plane_in,
    local_sem, q_send, q_recv, r_send, r_recv, h_send, h_recv,
):
    ax = lax.axis_index("ax")
    me = lax.axis_index("xs")
    held = part_ref.shape[1]
    (length_x, length_y, cores), offsets = peers_by_distance(n_xs)
    codes = [(dx * length_y + dy) * cores + core for dx, dy, core in offsets]

    loads = [
        pltpu.make_async_copy(source, target, local_sem.at[i])
        for i, (source, target) in enumerate(
            [
                (part_hbm, part_ref), (elem_hbm, elem_ref), (ref_hbm, ref_ref),
                (tau_hbm, tau_ref), (vel_hbm, vel_ref), (metric_hbm, metric_ref),
                (const_hbm, const_ref), (bvel_hbm, bvel_ref), (coef_hbm, coef_ref),
                (hist_hbm, hist_ref),
            ]
        )
    ]
    for load in loads[0:4]:
        load.start()

    def wrap(place, length):
        return jnp.where(place >= length, place - length, place)

    here_x = lax.div(me, length_y * cores)
    here_y = lax.rem(lax.div(me, cores), length_y)
    here_core = lax.rem(me, cores)
    places_x = [wrap(here_x + d, length_x) * (length_y * cores) for d in range(length_x)]
    places_y = [wrap(here_y + d, length_y) * cores for d in range(length_y)]
    places_core = [wrap(here_core + d, cores) for d in range(cores)]

    def ahead(place):
        dx, dy, core = offsets[place]
        return places_x[dx] + places_y[dy] + places_core[core]

    def behind(place):
        dx, dy, core = offsets[place]
        return (
            places_x[(length_x - dx) % length_x]
            + places_y[(length_y - dy) % length_y]
            + places_core[(cores - core) % cores]
        )

    up, down = wrap(ax + 1, n_ax), wrap(ax + n_ax - 1, n_ax)
    left, right = wrap(me + n_xs - 1, n_xs), wrap(me + 1, n_xs)

    barrier = pltpu.get_barrier_semaphore()
    for place in range(n_xs - 1, 0, -1):
        pl.semaphore_signal(barrier, inc=1, device_id=(ax, behind(place)), device_id_type=MESH)
    for other in (up, down):
        pl.semaphore_signal(barrier, inc=1, device_id=(other, me), device_id_type=MESH)

    def query_copy(first, count, group, target):
        return pltpu.make_async_remote_copy(
            src_ref=sendq.at[pl.ds(first, count), pl.ds(0, 5)],
            dst_ref=recvq.at[pl.ds(first, count), pl.ds(0, 5)],
            send_sem=q_send,
            recv_sem=q_recv.at[group],
            device_id=(ax, target),
            device_id_type=MESH,
        )

    def answer_copy(tile, count, odd, target):
        return pltpu.make_async_remote_copy(
            src_ref=sendr.at[pl.ds(tile, count), pl.ds(4 * odd, 3)],
            dst_ref=recvr.at[pl.ds(tile, count), pl.ds(4 * odd, 3)],
            send_sem=r_send.at[odd],
            recv_sem=r_recv.at[odd],
            device_id=(ax, target),
            device_id_type=MESH,
        )

    def face_copy(side):
        return pltpu.make_async_remote_copy(
            src_ref=face_out.at[side],
            dst_ref=face_in.at[side],
            send_sem=h_send.at[side],
            recv_sem=h_recv.at[side],
            device_id=(ax, right if side == 0 else left),
            device_id_type=MESH,
        )

    def plane_copy(side):
        return pltpu.make_async_remote_copy(
            src_ref=plane_out.at[side],
            dst_ref=plane_in.at[side],
            send_sem=h_send.at[2 + side],
            recv_sem=h_recv.at[2 + side],
            device_id=(up if side == 0 else down, me),
            device_id_type=MESH,
        )

    for load in loads[4:]:
        load.start()

    for load in loads[0:4]:
        load.wait()
    part = part_ref[...]
    far_x = part // (length_y * cores) - here_x
    far_y = (part // cores) % length_y - here_y
    far_core = part % cores - here_core
    rel = (
        jnp.where(far_x < 0, far_x + length_x, far_x) * (length_y * cores)
        + jnp.where(far_y < 0, far_y + length_y, far_y) * cores
        + jnp.where(far_core < 0, far_core + cores, far_core)
    )
    ranked(rel, n_xs, onehot)
    coords = jnp.concatenate([ref_ref[...], tau_ref[...]], axis=0)
    dispatch(rel, codes, coords, elem_ref[...].astype(F32), lhs, onehot, sendq, recvq)
    pl.semaphore_wait(barrier, n_xs + 1)
    for place in range(n_xs - 1, 0, -1):
        query_copy(place, 1, place // GROUP, ahead(place)).start()
    for load in loads[4:7]:
        load.wait()
    advection(vel_ref, metric_ref, const_ref, table, wsum)
    azimuth_pairs(wsum, face_out)
    for side in range(2):
        face_copy(side).start()

    groups = n_xs // GROUP
    middle = groups // 4
    order = list(range(middle, groups - 3))
    order += [g for g in range(groups - 1, -1, -1) if g not in order]
    for turn, group in enumerate(order):
        if turn == min(3, groups - 1):
            for side in range(2):
                face_copy(side).wait()
            add_faces(wsum, face_in, plane_out)
            for side in range(2):
                plane_copy(side).start()
        first = GROUP * group
        skip = 1 if group == 0 else 0
        query_copy(first + skip, GROUP - skip, group, me).wait_recv()
        sources = [recvq[first + i] for i in range(GROUP)]
        values = interpolate(jnp.concatenate(sources, axis=1), const_ref, table)
        for i in range(GROUP):
            place = first + i
            lanes = slice(SLOTS * i, SLOTS * (i + 1))
            target = sendr if place > 0 else recvr
            for comp in range(3):
                row = 4 * (place % 2) + comp
                target[place // 2, row : row + 1, :] = values[comp][:, lanes]
            if place > 0:
                answer_copy(place // 2, 1, place % 2, behind(place)).start()

    for load in loads[7:]:
        load.wait()
    quad = jnp.concatenate(
        [const_ref[ROW_QUAD + 8 * comp : ROW_QUAD + 8 * comp + 8, :] for comp in range(3)], axis=1
    )
    quad = jnp.concatenate([quad, jnp.zeros_like(quad)], axis=0).astype(BF16)
    basset = jnp.dot(quad, hist_ref[...], preferred_element_type=F32)[0:3]
    local = coef_ref[...] * basset - tau_ref[...] * bvel_ref[...]

    for side in range(2):
        plane_copy(side).wait()
    fluid_finish(wsum, plane_in, fluid_ref)
    store_fluid = pltpu.make_async_copy(fluid_ref, fluid_hbm, local_sem.at[len(loads)])
    store_fluid.start()

    query_copy(1, n_xs - 1, 0, me).wait_send()
    answer_copy(1, n_xs // 2 - 1, 0, me).wait()
    answer_copy(0, n_xs // 2, 1, me).wait()
    bubble_ref[...] = gather(rel, codes, recvr, onehot) + local
    store_fluid.wait()


def store(fluid_in, bubble_in, fluid_out, bubble_out, fluid_ref, bubble_ref, in_sems, out_sems):
    pieces = [(fluid_in.at[c], fluid_ref.at[c], fluid_out.at[c]) for c in range(3)]
    pieces.append((bubble_in, bubble_ref, bubble_out))
    reads = [pltpu.make_async_copy(p[0], p[1], in_sems.at[i]) for i, p in enumerate(pieces)]
    writes = [pltpu.make_async_copy(p[1], p[2], out_sems.at[i]) for i, p in enumerate(pieces)]
    for read in reads:
        read.start()
    for read, write in zip(reads, writes):
        read.wait()
        write.start()
    for write in writes:
        write.wait()


def shards(
    velocity, metric, bubble_part, bubble_elem, bubble_ref, bubble_vel, inv_tau,
    basset_coef, history,
):
    n_ax, n_xs = lax.axis_size("ax"), lax.axis_size("xs")
    held = bubble_part.shape[0]
    steps = history.shape[0]
    _, length_z, length_a, length_r = velocity.shape
    vmem = pl.BlockSpec(memory_space=pltpu.VMEM)
    anywhere = pl.BlockSpec(memory_space=pl.ANY)
    dma = pltpu.SemaphoreType.DMA
    outputs = (
        jax.ShapeDtypeStruct(velocity.shape, F32),
        jax.ShapeDtypeStruct((3, held), F32),
    )
    operands = [
        bubble_part.reshape(1, held),
        bubble_elem.reshape(1, held),
        bubble_ref,
        inv_tau.reshape(1, held),
        velocity,
        metric.reshape(3, length_a // 8, length_r // 8),
        jnp.asarray(constant_table(steps)),
        bubble_vel,
        basset_coef.reshape(1, held),
        history.transpose(1, 0, 2).reshape(3 * steps, held),
    ]
    results = pl.pallas_call(
        functools.partial(kernel, n_ax, n_xs),
        out_shape=outputs,
        in_specs=[anywhere] * len(operands),
        out_specs=(anywhere, vmem),
        scratch_shapes=[pltpu.VMEM(o.shape, o.dtype) for o in operands]
        + [
            pltpu.VMEM(velocity.shape, F32),
            pltpu.VMEM((16 * n_xs, held), BF16),
            pltpu.VMEM((SLOTS, held), BF16),
            pltpu.VMEM((n_xs, 8, SLOTS), F32),
            pltpu.VMEM((n_xs, 8, SLOTS), F32),
            pltpu.VMEM((n_xs // 2, 8, SLOTS), F32),
            pltpu.VMEM((n_xs // 2, 8, SLOTS), F32),
            pltpu.VMEM((6 * 64, 4 * length_r), BF16),
            pltpu.VMEM((4, length_z, length_a, length_r), F32),
            pltpu.VMEM((2, 4, length_z, length_r), F32),
            pltpu.VMEM((2, 4, length_z, length_r), F32),
            pltpu.VMEM((2, 4, length_a, length_r), F32),
            pltpu.VMEM((2, 4, length_a, length_r), F32),
            dma((len(operands) + 1,)),
            dma,
            dma((n_xs // GROUP,)),
            dma((2,)),
            dma((2,)),
            dma((4,)),
            dma((4,)),
        ],
        compiler_params=pltpu.CompilerParams(
            collective_id=0, has_side_effects=True, vmem_limit_bytes=56 * 1024 * 1024
        ),
    )(*operands)
    return pl.pallas_call(
        store,
        out_shape=outputs,
        in_specs=[anywhere, anywhere],
        out_specs=(anywhere, anywhere),
        scratch_shapes=[pltpu.VMEM(o.shape, o.dtype) for o in outputs] + [dma((4,)), dma((4,))],
        compiler_params=pltpu.CompilerParams(vmem_limit_bytes=56 * 1024 * 1024),
    )(*results)


def solution(mesh):
    return jax.shard_map(
        shards,
        mesh=mesh,
        in_specs=(
            P(None, "ax", "xs", None),
            P(None, "ax", "xs", None),
            P(("ax", "xs")),
            P(("ax", "xs")),
            P(None, ("ax", "xs")),
            P(None, ("ax", "xs")),
            P(("ax", "xs")),
            P(("ax", "xs")),
            P(None, None, ("ax", "xs")),
        ),
        out_specs=(P(None, "ax", "xs", None), P(None, ("ax", "xs"))),
        check_vma=False,
    )
```

```python
import functools

import jax
import jax.numpy as jnp
import numpy as np
from jax import lax
from jax.experimental import pallas as pl
from jax.experimental.pallas import tpu as pltpu
from jax.sharding import PartitionSpec as P

GLL_POINTS = (
    -1.0,
    -0.8717401485096066,
    -0.5917001814331423,
    -0.2092992179024789,
    0.2092992179024789,
    0.5917001814331423,
    0.8717401485096066,
    1.0,
)
GLL_WEIGHTS = (
    0.03571428571428571,
    0.21070422714350603,
    0.34112269248350435,
    0.4124587946587039,
    0.4124587946587039,
    0.34112269248350435,
    0.21070422714350603,
    0.03571428571428571,
)
SLOTS = 128
GROUP = 4
MESH = pl.DeviceIdType.MESH
F32 = jnp.float32
BF16 = jnp.bfloat16


def derivative_matrix():
    points = np.array(GLL_POINTS)
    identity = np.eye(8)
    spread = points[:, None] - points[None, :] + identity
    products = np.prod(spread, axis=1)
    matrix = products[:, None] / products[None, :] / spread
    off_diagonal = matrix * (1.0 - identity)
    return off_diagonal - identity * off_diagonal.sum(axis=1)[:, None]


DMAT = derivative_matrix()

ROW_POINT = 0
ROW_NORM = 8
ROW_ROLL = 16
ROW_WEIGHT = 80
ROW_RADIAL = 112
ROW_QUAD = 240


def constant_table(steps):
    points = np.array(GLL_POINTS)
    weights = np.array(GLL_WEIGHTS)
    rows = [np.repeat(points[:, None], 128, axis=1)]
    spread = points[:, None] - points[None, :] + np.eye(8)
    rows.append(np.repeat((1.0 / np.prod(spread, axis=1))[:, None], 128, axis=1))
    for shift in range(8):
        coef = np.array([DMAT[i, (i - shift) % 8] for i in range(8)])
        rows.append(np.repeat(coef[:, None], 128, axis=1))
    rows.append(np.tile(weights, 4)[:, None] * np.tile(weights, 16)[None, :])
    rows.append(np.kron(np.eye(16), DMAT.T))
    rows += quadrature_rows(steps)
    return np.concatenate(rows, axis=0).astype(np.float32)


def quadrature_rows(length):
    steps = np.arange(length, dtype=np.float32)
    quad = np.sqrt(steps + np.float32(1.0)) - np.sqrt(steps)
    rows = np.zeros((3, 8, length), np.float32)
    for comp in range(3):
        rows[comp, comp] = quad
    return list(rows)


def peers_by_distance(n_xs):
    length_x, length_y, cores = {32: (4, 4, 2), 4: (2, 1, 2)}[n_xs]
    offsets = [
        (dx, dy, core)
        for dx in range(length_x)
        for dy in range(length_y)
        for core in range(cores)
    ]

    def distance(offset):
        return min(offset[0], length_x - offset[0]) + min(offset[1], length_y - offset[1])

    return (length_x, length_y, cores), sorted(offsets, key=distance)


def split3(values):
    high = values.astype(BF16).astype(F32)
    rest = values - high
    mid = rest.astype(BF16).astype(F32)
    return high, mid, rest - mid


def ranked(rel, n_xs, onehot):
    held = rel.shape[1]
    member = (
        jnp.broadcast_to(rel, (n_xs, held))
        == lax.broadcasted_iota(jnp.int32, (n_xs, held), 0)
    ).astype(F32)
    chunks = held // 128
    pieces = [member[:, c * 128 : (c + 1) * 128] for c in range(chunks)]
    stacked = jnp.concatenate(pieces, axis=0).astype(BF16)
    before = (
        lax.broadcasted_iota(jnp.int32, (128, 128), 0)
        < lax.broadcasted_iota(jnp.int32, (128, 128), 1)
    ).astype(F32).astype(BF16)
    counts = jnp.dot(stacked, before, preferred_element_type=F32)
    totals = jnp.dot(stacked, jnp.ones((128, 128), BF16), preferred_element_type=F32)
    carry = jnp.zeros((n_xs, 128), F32)
    ranks = []
    for c in range(chunks):
        rows = slice(c * n_xs, (c + 1) * n_xs)
        ranks.append(jnp.sum(pieces[c] * (counts[rows] + carry), axis=0, keepdims=True))
        carry = carry + totals[rows]
    rank = jnp.concatenate(ranks, axis=1).astype(jnp.int32)
    onehot[...] = (
        jnp.broadcast_to(rank, (SLOTS, held))
        == lax.broadcasted_iota(jnp.int32, (SLOTS, held), 0)
    ).astype(F32).astype(BF16)


def dispatch(rel, codes, coords, elem, lhs, onehot, sendq, recvq):
    held = rel.shape[1]
    high, mid, low = split3(coords)
    packed = jnp.concatenate(
        [high, elem, jnp.zeros((3, held), F32), mid, low], axis=0
    ).astype(BF16)
    rel16 = jnp.broadcast_to(rel, (16, held))
    zero = jnp.zeros((16, held), BF16)
    n_xs = len(codes)
    for place, code in enumerate(codes):
        lhs[16 * place : 16 * place + 16, :] = jnp.where(rel16 == code, packed, zero)
    slots = lax.dot_general(
        lhs[...], onehot[...], (((1,), (1,)), ((), ())), preferred_element_type=F32
    ).reshape(n_xs, 2, 8, SLOTS)
    rest = slots[:, 1]
    rest = rest + pltpu.roll(rest, 4, 1)
    row = lax.broadcasted_iota(jnp.int32, (n_xs, 8, SLOTS), 1)
    slots = slots[:, 0] + jnp.where(row < 4, rest, 0.0)
    sendq[...] = slots
    recvq[0] = slots[0]


def advection(vel_ref, metric_ref, const_ref, table, wsum):
    vel = vel_ref[...]
    length_a, length_r = vel.shape[2], vel.shape[3]
    nodes = 8 * length_a
    grad_r = jnp.dot(
        vel.reshape(3 * nodes, length_r),
        const_ref[ROW_RADIAL : ROW_RADIAL + 128, :],
        preferred_element_type=F32,
        precision=lax.Precision.HIGHEST,
    ).reshape(vel.shape)
    spread = (
        lax.broadcasted_iota(jnp.int32, (length_r // 8, length_r), 1) // 8
        == lax.broadcasted_iota(jnp.int32, (length_r // 8, length_r), 0)
    ).astype(F32)
    scale = []
    for factor in range(3):
        rows = jnp.dot(
            metric_ref[factor], spread, preferred_element_type=F32, precision=lax.Precision.HIGHEST
        )
        scale.append(
            jnp.concatenate(
                [
                    jnp.broadcast_to(rows[e : e + 1], (8, length_r))
                    for e in range(length_a // 8)
                ],
                axis=0,
            )
        )
    inverse = const_ref[ROW_WEIGHT : ROW_WEIGHT + 32, :] / (scale[0] * scale[1] * scale[2])
    lane = lax.broadcasted_iota(jnp.int32, (4, length_a, length_r), 2)
    upper = (lane % 8 == 7) & (lane < length_r - 1)
    lower = (lane % 8 == 0) & (lane > 0)
    for z in range(8):
        here = vel[:, z]
        grad_z = sum(float(DMAT[z, j]) * vel[:, j] for j in range(8) if abs(DMAT[z, j]) > 1e-9)
        groups = here.reshape(3 * length_a // 8, 8, length_r)
        grad_a = const_ref[ROW_ROLL : ROW_ROLL + 8, :] * groups
        for shift in range(1, 8):
            coef = const_ref[ROW_ROLL + 8 * shift : ROW_ROLL + 8 * shift + 8, :]
            grad_a = grad_a + coef * pltpu.roll(groups, shift, 1)
        grad_a = grad_a.reshape(here.shape)
        advect = (
            (here[0] * scale[0])[None] * grad_z
            + (here[1] * scale[1])[None] * grad_a
            + (here[2] * scale[2])[None] * grad_r[:, z]
        )
        fields = [here[0], here[1], here[2], advect[0], advect[1], advect[2]]
        if z % 2 == 1:
            for field in range(6):
                for element in range(length_a // 8):
                    rows = slice(8 * element, 8 * element + 8)
                    pair = jnp.concatenate([earlier[field][rows], fields[field][rows]], axis=0)
                    table[
                        64 * field + 8 * (z - 1) : 64 * field + 8 * (z + 1),
                        length_r * element : length_r * (element + 1),
                    ] = pair.astype(BF16)
        earlier = fields
        mass = GLL_WEIGHTS[z] * inverse
        weighted = jnp.concatenate([mass[None] * advect, mass[None]], axis=0)
        after = pltpu.roll(weighted, length_r - 1, 2)
        prior = pltpu.roll(weighted, 1, 2)
        wsum[:, z] = weighted + jnp.where(upper, after, jnp.where(lower, prior, 0.0))


def azimuth_pairs(wsum, face_out):
    length_a = wsum.shape[2]
    for edge in range(8, length_a, 8):
        both = wsum[:, :, edge - 1 : edge, :] + wsum[:, :, edge : edge + 1, :]
        wsum[:, :, edge - 1 : edge, :] = both
        wsum[:, :, edge : edge + 1, :] = both
    for z in range(8):
        face_out[0, :, z : z + 1, :] = wsum[:, z, length_a - 1 : length_a, :]
        face_out[1, :, z : z + 1, :] = wsum[:, z, 0:1, :]


def add_faces(wsum, face_in, plane_out):
    length_a = wsum.shape[2]
    last = slice(length_a - 1, length_a)
    for z in range(8):
        wsum[:, z, 0:1, :] = wsum[:, z, 0:1, :] + face_in[0, :, z : z + 1, :]
        wsum[:, z, last, :] = wsum[:, z, last, :] + face_in[1, :, z : z + 1, :]
    plane_out[0] = wsum[:, 7]
    plane_out[1] = wsum[:, 0]


def fluid_finish(wsum, plane_in, fluid_ref):
    for z in range(8):
        total = wsum[:, z]
        if z == 0:
            total = total + plane_in[0]
        if z == 7:
            total = total + plane_in[1]
        fluid_ref[:, z] = total[0:3] * (-1.0 / total[3:4])


def interpolate(both, const_ref, table):
    width = both.shape[1]
    point = jnp.concatenate([const_ref[ROW_POINT : ROW_POINT + 8, :]] * (width // 128), axis=1)
    norm = jnp.concatenate([const_ref[ROW_NORM : ROW_NORM + 8, :]] * (width // 128), axis=1)

    def lagrange(row):
        diff = row - point
        one = pltpu.roll(diff, 1, 0)
        two = one * pltpu.roll(one, 1, 0)
        four = two * pltpu.roll(two, 2, 0)
        rest = four * pltpu.roll(two, 4, 0) * pltpu.roll(one, 6, 0)
        return (rest * norm).astype(BF16).astype(F32)

    lag_z = lagrange(both[0:1])
    lag_a = lagrange(both[1:2])
    lag_r = lagrange(both[2:3])
    tau = both[3:4]
    element = both[4:5].astype(jnp.int32)
    radial = jnp.broadcast_to(element & 15, (8, width))
    azimuth = jnp.broadcast_to((element >> 4) & 3, (128, width))
    weight_r = jnp.concatenate(
        [jnp.where(radial == e, lag_r, 0.0) for e in range(16)], axis=0
    ).astype(BF16)
    zero = jnp.zeros_like(weight_r)
    weight = jnp.concatenate(
        [jnp.where(azimuth == e, weight_r, zero) for e in range(4)], axis=0
    )
    first = jnp.dot(table[...], weight, preferred_element_type=F32)
    sums = []
    for field in range(6):
        total = jnp.zeros((8, width), F32)
        for z in range(8):
            row = 64 * field + 8 * z
            total = total + first[row : row + 8] * lag_z[z : z + 1]
        sums.append(total * lag_a)
    return [
        jnp.sum(3.0 * sums[3 + comp] + tau * sums[comp], axis=0, keepdims=True)
        for comp in range(3)
    ]


def gather(rel, codes, recvr, onehot):
    held = rel.shape[1]
    n_xs = len(codes)
    rel8 = jnp.broadcast_to(rel, (8, held))
    answers = recvr[...].reshape(4 * n_xs, SLOTS)
    spread = jnp.dot(
        jnp.concatenate([p.astype(BF16) for p in split3(answers)], axis=0),
        onehot[...],
        preferred_element_type=F32,
    )
    span = 4 * n_xs
    half = lax.broadcasted_iota(jnp.int32, (8, held), 0) < 4
    total = jnp.zeros((8, held), F32)
    for pair in range(n_xs // 2):
        rows = [spread[w * span + 8 * pair : w * span + 8 * pair + 8] for w in range(3)]
        code = jnp.where(half, codes[2 * pair], codes[2 * pair + 1])
        total = total + jnp.where(rel8 == code, rows[0] + rows[1] + rows[2], 0.0)
    total = total + pltpu.roll(total, 4, 0)
    return total[0:3]


def kernel(
    n_ax, n_xs,
    part_hbm, elem_hbm, ref_hbm, tau_hbm, vel_hbm, metric_hbm, const_hbm, bvel_hbm, coef_hbm,
    hist_hbm,
    fluid_hbm, bubble_ref,
    part_ref, elem_ref, ref_ref, tau_ref, vel_ref, metric_ref, const_ref, bvel_ref, coef_ref,
    hist_ref,
    fluid_ref, lhs, onehot, sendq, recvq, sendr, recvr, table, wsum, face_out, face_in, plane_out, plane_in,
    local_sem, q_send, q_recv, r_send, r_recv, h_send, h_recv,
):
    ax = lax.axis_index("ax")
    me = lax.axis_index("xs")
    held = part_ref.shape[1]
    (length_x, length_y, cores), offsets = peers_by_distance(n_xs)
    codes = [(dx * length_y + dy) * cores + core for dx, dy, core in offsets]

    loads = [
        pltpu.make_async_copy(source, target, local_sem.at[i])
        for i, (source, target) in enumerate(
            [
                (part_hbm, part_ref), (elem_hbm, elem_ref), (ref_hbm, ref_ref),
                (tau_hbm, tau_ref), (vel_hbm, vel_ref), (metric_hbm, metric_ref),
                (const_hbm, const_ref), (bvel_hbm, bvel_ref), (coef_hbm, coef_ref),
                (hist_hbm, hist_ref),
            ]
        )
    ]
    def wrap(place, length):
        return jnp.where(place >= length, place - length, place)

    here_x = lax.div(me, length_y * cores)
    here_y = lax.rem(lax.div(me, cores), length_y)
    here_core = lax.rem(me, cores)
    places_x = [wrap(here_x + d, length_x) * (length_y * cores) for d in range(length_x)]
    places_y = [wrap(here_y + d, length_y) * cores for d in range(length_y)]
    places_core = [wrap(here_core + d, cores) for d in range(cores)]

    def ahead(place):
        dx, dy, core = offsets[place]
        return places_x[dx] + places_y[dy] + places_core[core]

    def behind(place):
        dx, dy, core = offsets[place]
        return (
            places_x[(length_x - dx) % length_x]
            + places_y[(length_y - dy) % length_y]
            + places_core[(cores - core) % cores]
        )

    up, down = wrap(ax + 1, n_ax), wrap(ax + n_ax - 1, n_ax)
    left, right = wrap(me + n_xs - 1, n_xs), wrap(me + 1, n_xs)

    barrier = pltpu.get_barrier_semaphore()
    for other in (up, down):
        pl.semaphore_signal(barrier, inc=1, device_id=(other, me), device_id_type=MESH)
    for place in range(n_xs - 1, 0, -1):
        pl.semaphore_signal(barrier, inc=1, device_id=(ax, behind(place)), device_id_type=MESH)

    def query_copy(first, count, group, target):
        return pltpu.make_async_remote_copy(
            src_ref=sendq.at[pl.ds(first, count), pl.ds(0, 5)],
            dst_ref=recvq.at[pl.ds(first, count), pl.ds(0, 5)],
            send_sem=q_send,
            recv_sem=q_recv.at[group],
            device_id=(ax, target),
            device_id_type=MESH,
        )

    def answer_copy(tile, count, odd, target):
        return pltpu.make_async_remote_copy(
            src_ref=sendr.at[pl.ds(tile, count), pl.ds(4 * odd, 3)],
            dst_ref=recvr.at[pl.ds(tile, count), pl.ds(4 * odd, 3)],
            send_sem=r_send.at[odd],
            recv_sem=r_recv.at[odd],
            device_id=(ax, target),
            device_id_type=MESH,
        )

    def face_copy(side):
        return pltpu.make_async_remote_copy(
            src_ref=face_out.at[side],
            dst_ref=face_in.at[side],
            send_sem=h_send.at[side],
            recv_sem=h_recv.at[side],
            device_id=(ax, right if side == 0 else left),
            device_id_type=MESH,
        )

    def plane_copy(side):
        return pltpu.make_async_remote_copy(
            src_ref=plane_out.at[side],
            dst_ref=plane_in.at[side],
            send_sem=h_send.at[2 + side],
            recv_sem=h_recv.at[2 + side],
            device_id=(up if side == 0 else down, me),
            device_id_type=MESH,
        )

    for load in loads:
        load.start()

    for load in loads[0:4]:
        load.wait()
    part = part_ref[...]
    far_x = part // (length_y * cores) - here_x
    far_y = (part // cores) % length_y - here_y
    far_core = part % cores - here_core
    rel = (
        jnp.where(far_x < 0, far_x + length_x, far_x) * (length_y * cores)
        + jnp.where(far_y < 0, far_y + length_y, far_y) * cores
        + jnp.where(far_core < 0, far_core + cores, far_core)
    )
    ranked(rel, n_xs, onehot)
    coords = jnp.concatenate([ref_ref[...], tau_ref[...]], axis=0)
    dispatch(rel, codes, coords, elem_ref[...].astype(F32), lhs, onehot, sendq, recvq)
    pl.semaphore_wait(barrier, n_xs + 1)
    for place in range(n_xs - 1, 0, -1):
        query_copy(place, 1, place // GROUP, ahead(place)).start()
    for load in loads[4:7]:
        load.wait()
    advection(vel_ref, metric_ref, const_ref, table, wsum)
    azimuth_pairs(wsum, face_out)
    for side in range(2):
        face_copy(side).start()

    groups = n_xs // GROUP
    middle = groups // 4
    order = list(range(middle, groups - 3))
    order += [g for g in range(groups - 1, -1, -1) if g not in order]
    for turn, group in enumerate(order):
        if turn == min(3, groups - 1):
            for side in range(2):
                face_copy(side).wait()
            add_faces(wsum, face_in, plane_out)
            for side in range(2):
                plane_copy(side).start()
        first = GROUP * group
        skip = 1 if group == 0 else 0
        query_copy(first + skip, GROUP - skip, group, me).wait_recv()
        sources = [recvq[first + i] for i in range(GROUP)]
        values = interpolate(jnp.concatenate(sources, axis=1), const_ref, table)
        for i in range(GROUP):
            place = first + i
            lanes = slice(SLOTS * i, SLOTS * (i + 1))
            target = sendr if place > 0 else recvr
            for comp in range(3):
                row = 4 * (place % 2) + comp
                target[place // 2, row : row + 1, :] = values[comp][:, lanes]
            if place > 0:
                answer_copy(place // 2, 1, place % 2, behind(place)).start()

    for load in loads[7:]:
        load.wait()
    quad = jnp.concatenate(
        [const_ref[ROW_QUAD + 8 * comp : ROW_QUAD + 8 * comp + 8, :] for comp in range(3)], axis=1
    )
    quad = jnp.concatenate([quad, jnp.zeros_like(quad)], axis=0).astype(BF16)
    basset = jnp.dot(quad, hist_ref[...], preferred_element_type=F32)[0:3]
    local = coef_ref[...] * basset - tau_ref[...] * bvel_ref[...]

    for side in range(2):
        plane_copy(side).wait()
    fluid_finish(wsum, plane_in, fluid_ref)
    store_fluid = pltpu.make_async_copy(fluid_ref, fluid_hbm, local_sem.at[len(loads)])
    store_fluid.start()

    query_copy(1, n_xs - 1, 0, me).wait_send()
    answer_copy(1, n_xs // 2 - 1, 0, me).wait()
    answer_copy(0, n_xs // 2, 1, me).wait()
    bubble_ref[...] = gather(rel, codes, recvr, onehot) + local
    store_fluid.wait()


def store(fluid_in, bubble_in, fluid_out, bubble_out, fluid_ref, bubble_ref, in_sems, out_sems):
    pieces = [(fluid_in.at[c], fluid_ref.at[c], fluid_out.at[c]) for c in range(3)]
    pieces.append((bubble_in, bubble_ref, bubble_out))
    reads = [pltpu.make_async_copy(p[0], p[1], in_sems.at[i]) for i, p in enumerate(pieces)]
    writes = [pltpu.make_async_copy(p[1], p[2], out_sems.at[i]) for i, p in enumerate(pieces)]
    for read in reads:
        read.start()
    for read, write in zip(reads, writes):
        read.wait()
        write.start()
    for write in writes:
        write.wait()


def shards(
    velocity, metric, bubble_part, bubble_elem, bubble_ref, bubble_vel, inv_tau,
    basset_coef, history,
):
    n_ax, n_xs = lax.axis_size("ax"), lax.axis_size("xs")
    held = bubble_part.shape[0]
    steps = history.shape[0]
    _, length_z, length_a, length_r = velocity.shape
    vmem = pl.BlockSpec(memory_space=pltpu.VMEM)
    anywhere = pl.BlockSpec(memory_space=pl.ANY)
    dma = pltpu.SemaphoreType.DMA
    outputs = (
        jax.ShapeDtypeStruct(velocity.shape, F32),
        jax.ShapeDtypeStruct((3, held), F32),
    )
    operands = [
        bubble_part.reshape(1, held),
        bubble_elem.reshape(1, held),
        bubble_ref,
        inv_tau.reshape(1, held),
        velocity,
        metric.reshape(3, length_a // 8, length_r // 8),
        jnp.asarray(constant_table(steps)),
        bubble_vel,
        basset_coef.reshape(1, held),
        history.transpose(1, 0, 2).reshape(3 * steps, held),
    ]
    results = pl.pallas_call(
        functools.partial(kernel, n_ax, n_xs),
        out_shape=outputs,
        in_specs=[anywhere] * len(operands),
        out_specs=(anywhere, vmem),
        scratch_shapes=[pltpu.VMEM(o.shape, o.dtype) for o in operands]
        + [
            pltpu.VMEM(velocity.shape, F32),
            pltpu.VMEM((16 * n_xs, held), BF16),
            pltpu.VMEM((SLOTS, held), BF16),
            pltpu.VMEM((n_xs, 8, SLOTS), F32),
            pltpu.VMEM((n_xs, 8, SLOTS), F32),
            pltpu.VMEM((n_xs // 2, 8, SLOTS), F32),
            pltpu.VMEM((n_xs // 2, 8, SLOTS), F32),
            pltpu.VMEM((6 * 64, 4 * length_r), BF16),
            pltpu.VMEM((4, length_z, length_a, length_r), F32),
            pltpu.VMEM((2, 4, length_z, length_r), F32),
            pltpu.VMEM((2, 4, length_z, length_r), F32),
            pltpu.VMEM((2, 4, length_a, length_r), F32),
            pltpu.VMEM((2, 4, length_a, length_r), F32),
            dma((len(operands) + 1,)),
            dma,
            dma((n_xs // GROUP,)),
            dma((2,)),
            dma((2,)),
            dma((4,)),
            dma((4,)),
        ],
        compiler_params=pltpu.CompilerParams(
            collective_id=0, has_side_effects=True, vmem_limit_bytes=56 * 1024 * 1024
        ),
    )(*operands)
    return pl.pallas_call(
        store,
        out_shape=outputs,
        in_specs=[anywhere, anywhere],
        out_specs=(anywhere, anywhere),
        scratch_shapes=[pltpu.VMEM(o.shape, o.dtype) for o in outputs] + [dma((4,)), dma((4,))],
        compiler_params=pltpu.CompilerParams(vmem_limit_bytes=56 * 1024 * 1024),
    )(*results)


def solution(mesh):
    return jax.shard_map(
        shards,
        mesh=mesh,
        in_specs=(
            P(None, "ax", "xs", None),
            P(None, "ax", "xs", None),
            P(("ax", "xs")),
            P(("ax", "xs")),
            P(None, ("ax", "xs")),
            P(None, ("ax", "xs")),
            P(("ax", "xs")),
            P(("ax", "xs")),
            P(None, None, ("ax", "xs")),
        ),
        out_specs=(P(None, "ax", "xs", None), P(None, ("ax", "xs"))),
        check_vma=False,
    )
```

```python
import functools

import jax
import jax.numpy as jnp
import numpy as np
from jax import lax
from jax.experimental import pallas as pl
from jax.experimental.pallas import tpu as pltpu
from jax.sharding import PartitionSpec as P

GLL_POINTS = (
    -1.0,
    -0.8717401485096066,
    -0.5917001814331423,
    -0.2092992179024789,
    0.2092992179024789,
    0.5917001814331423,
    0.8717401485096066,
    1.0,
)
GLL_WEIGHTS = (
    0.03571428571428571,
    0.21070422714350603,
    0.34112269248350435,
    0.4124587946587039,
    0.4124587946587039,
    0.34112269248350435,
    0.21070422714350603,
    0.03571428571428571,
)
SLOTS = 128
GROUP = 4
MESH = pl.DeviceIdType.MESH
F32 = jnp.float32
BF16 = jnp.bfloat16


def derivative_matrix():
    points = np.array(GLL_POINTS)
    identity = np.eye(8)
    spread = points[:, None] - points[None, :] + identity
    products = np.prod(spread, axis=1)
    matrix = products[:, None] / products[None, :] / spread
    off_diagonal = matrix * (1.0 - identity)
    return off_diagonal - identity * off_diagonal.sum(axis=1)[:, None]


DMAT = derivative_matrix()

ROW_POINT = 0
ROW_NORM = 8
ROW_ROLL = 16
ROW_WEIGHT = 80
ROW_RADIAL = 112
ROW_QUAD = 240


def constant_table(steps):
    points = np.array(GLL_POINTS)
    weights = np.array(GLL_WEIGHTS)
    rows = [np.repeat(points[:, None], 128, axis=1)]
    spread = points[:, None] - points[None, :] + np.eye(8)
    rows.append(np.repeat((1.0 / np.prod(spread, axis=1))[:, None], 128, axis=1))
    for shift in range(8):
        coef = np.array([DMAT[i, (i - shift) % 8] for i in range(8)])
        rows.append(np.repeat(coef[:, None], 128, axis=1))
    rows.append(np.tile(weights, 4)[:, None] * np.tile(weights, 16)[None, :])
    rows.append(np.kron(np.eye(16), DMAT.T))
    rows += quadrature_rows(steps)
    return np.concatenate(rows, axis=0).astype(np.float32)


def quadrature_rows(length):
    steps = np.arange(length, dtype=np.float32)
    quad = np.sqrt(steps + np.float32(1.0)) - np.sqrt(steps)
    rows = np.zeros((3, 8, length), np.float32)
    for comp in range(3):
        rows[comp, comp] = quad
    return list(rows)


def peers_by_distance(n_xs):
    length_x, length_y, cores = {32: (4, 4, 2), 4: (2, 1, 2)}[n_xs]
    offsets = [
        (dx, dy, core)
        for dx in range(length_x)
        for dy in range(length_y)
        for core in range(cores)
    ]

    def distance(offset):
        return min(offset[0], length_x - offset[0]) + min(offset[1], length_y - offset[1])

    return (length_x, length_y, cores), sorted(offsets, key=distance)


def split3(values):
    high = values.astype(BF16).astype(F32)
    rest = values - high
    mid = rest.astype(BF16).astype(F32)
    return high, mid, rest - mid


def ranked(rel, n_xs, onehot):
    held = rel.shape[1]
    member = (
        jnp.broadcast_to(rel, (n_xs, held))
        == lax.broadcasted_iota(jnp.int32, (n_xs, held), 0)
    ).astype(F32)
    chunks = held // 128
    pieces = [member[:, c * 128 : (c + 1) * 128] for c in range(chunks)]
    stacked = jnp.concatenate(pieces, axis=0).astype(BF16)
    before = (
        lax.broadcasted_iota(jnp.int32, (128, 128), 0)
        < lax.broadcasted_iota(jnp.int32, (128, 128), 1)
    ).astype(F32).astype(BF16)
    counts = jnp.dot(stacked, before, preferred_element_type=F32)
    totals = jnp.dot(stacked, jnp.ones((128, 128), BF16), preferred_element_type=F32)
    carry = jnp.zeros((n_xs, 128), F32)
    ranks = []
    for c in range(chunks):
        rows = slice(c * n_xs, (c + 1) * n_xs)
        ranks.append(jnp.sum(pieces[c] * (counts[rows] + carry), axis=0, keepdims=True))
        carry = carry + totals[rows]
    rank = jnp.concatenate(ranks, axis=1).astype(jnp.int32)
    onehot[...] = (
        jnp.broadcast_to(rank, (SLOTS, held))
        == lax.broadcasted_iota(jnp.int32, (SLOTS, held), 0)
    ).astype(F32).astype(BF16)


def dispatch(rel, codes, coords, elem, lhs, onehot, sendq, recvq):
    held = rel.shape[1]
    high, mid, low = split3(coords)
    packed = jnp.concatenate(
        [high, elem, jnp.zeros((3, held), F32), mid, low], axis=0
    ).astype(BF16)
    rel16 = jnp.broadcast_to(rel, (16, held))
    zero = jnp.zeros((16, held), BF16)
    n_xs = len(codes)
    for place, code in enumerate(codes):
        lhs[16 * place : 16 * place + 16, :] = jnp.where(rel16 == code, packed, zero)
    slots = lax.dot_general(
        lhs[...], onehot[...], (((1,), (1,)), ((), ())), preferred_element_type=F32
    ).reshape(n_xs, 2, 8, SLOTS)
    rest = slots[:, 1]
    rest = rest + pltpu.roll(rest, 4, 1)
    row = lax.broadcasted_iota(jnp.int32, (n_xs, 8, SLOTS), 1)
    slots = slots[:, 0] + jnp.where(row < 4, rest, 0.0)
    sendq[...] = slots
    recvq[0] = slots[0]


def advection(vel_ref, metric_ref, const_ref, table, wsum):
    vel = vel_ref[...]
    length_a, length_r = vel.shape[2], vel.shape[3]
    nodes = 8 * length_a
    grad_r = jnp.dot(
        vel.reshape(3 * nodes, length_r),
        const_ref[ROW_RADIAL : ROW_RADIAL + 128, :],
        preferred_element_type=F32,
        precision=lax.Precision.HIGHEST,
    ).reshape(vel.shape)
    spread = (
        lax.broadcasted_iota(jnp.int32, (length_r // 8, length_r), 1) // 8
        == lax.broadcasted_iota(jnp.int32, (length_r // 8, length_r), 0)
    ).astype(F32)
    scale = []
    for factor in range(3):
        rows = jnp.dot(
            metric_ref[factor], spread, preferred_element_type=F32, precision=lax.Precision.HIGHEST
        )
        scale.append(
            jnp.concatenate(
                [
                    jnp.broadcast_to(rows[e : e + 1], (8, length_r))
                    for e in range(length_a // 8)
                ],
                axis=0,
            )
        )
    inverse = const_ref[ROW_WEIGHT : ROW_WEIGHT + 32, :] / (scale[0] * scale[1] * scale[2])
    lane = lax.broadcasted_iota(jnp.int32, (4, length_a, length_r), 2)
    upper = (lane % 8 == 7) & (lane < length_r - 1)
    lower = (lane % 8 == 0) & (lane > 0)
    for z in range(8):
        here = vel[:, z]
        grad_z = sum(float(DMAT[z, j]) * vel[:, j] for j in range(8) if abs(DMAT[z, j]) > 1e-9)
        groups = here.reshape(3 * length_a // 8, 8, length_r)
        grad_a = const_ref[ROW_ROLL : ROW_ROLL + 8, :] * groups
        for shift in range(1, 8):
            coef = const_ref[ROW_ROLL + 8 * shift : ROW_ROLL + 8 * shift + 8, :]
            grad_a = grad_a + coef * pltpu.roll(groups, shift, 1)
        grad_a = grad_a.reshape(here.shape)
        advect = (
            (here[0] * scale[0])[None] * grad_z
            + (here[1] * scale[1])[None] * grad_a
            + (here[2] * scale[2])[None] * grad_r[:, z]
        )
        fields = [here[0], here[1], here[2], advect[0], advect[1], advect[2]]
        if z % 2 == 1:
            for field in range(6):
                for element in range(length_a // 8):
                    rows = slice(8 * element, 8 * element + 8)
                    pair = jnp.concatenate([earlier[field][rows], fields[field][rows]], axis=0)
                    table[
                        64 * field + 8 * (z - 1) : 64 * field + 8 * (z + 1),
                        length_r * element : length_r * (element + 1),
                    ] = pair.astype(BF16)
        earlier = fields
        mass = GLL_WEIGHTS[z] * inverse
        weighted = jnp.concatenate([mass[None] * advect, mass[None]], axis=0)
        after = pltpu.roll(weighted, length_r - 1, 2)
        prior = pltpu.roll(weighted, 1, 2)
        wsum[:, z] = weighted + jnp.where(upper, after, jnp.where(lower, prior, 0.0))


def azimuth_pairs(wsum, face_out):
    length_a = wsum.shape[2]
    for edge in range(8, length_a, 8):
        both = wsum[:, :, edge - 1 : edge, :] + wsum[:, :, edge : edge + 1, :]
        wsum[:, :, edge - 1 : edge, :] = both
        wsum[:, :, edge : edge + 1, :] = both
    for z in range(8):
        face_out[0, :, z : z + 1, :] = wsum[:, z, length_a - 1 : length_a, :]
        face_out[1, :, z : z + 1, :] = wsum[:, z, 0:1, :]


def add_faces(wsum, face_in, plane_out):
    length_a = wsum.shape[2]
    last = slice(length_a - 1, length_a)
    for z in range(8):
        wsum[:, z, 0:1, :] = wsum[:, z, 0:1, :] + face_in[0, :, z : z + 1, :]
        wsum[:, z, last, :] = wsum[:, z, last, :] + face_in[1, :, z : z + 1, :]
    plane_out[0] = wsum[:, 7]
    plane_out[1] = wsum[:, 0]


def fluid_finish(wsum, plane_in, fluid_ref):
    for z in range(8):
        total = wsum[:, z]
        if z == 0:
            total = total + plane_in[0]
        if z == 7:
            total = total + plane_in[1]
        fluid_ref[:, z] = total[0:3] * (-1.0 / total[3:4])


def interpolate(both, const_ref, table):
    width = both.shape[1]
    point = jnp.concatenate([const_ref[ROW_POINT : ROW_POINT + 8, :]] * (width // 128), axis=1)
    norm = jnp.concatenate([const_ref[ROW_NORM : ROW_NORM + 8, :]] * (width // 128), axis=1)

    def lagrange(row):
        diff = row - point
        one = pltpu.roll(diff, 1, 0)
        two = one * pltpu.roll(one, 1, 0)
        four = two * pltpu.roll(two, 2, 0)
        rest = four * pltpu.roll(two, 4, 0) * pltpu.roll(one, 6, 0)
        return (rest * norm).astype(BF16).astype(F32)

    lag_z = lagrange(both[0:1])
    lag_a = lagrange(both[1:2])
    lag_r = lagrange(both[2:3])
    tau = both[3:4]
    element = both[4:5].astype(jnp.int32)
    radial = jnp.broadcast_to(element & 15, (8, width))
    azimuth = jnp.broadcast_to((element >> 4) & 3, (128, width))
    weight_r = jnp.concatenate(
        [jnp.where(radial == e, lag_r, 0.0) for e in range(16)], axis=0
    ).astype(BF16)
    zero = jnp.zeros_like(weight_r)
    weight = jnp.concatenate(
        [jnp.where(azimuth == e, weight_r, zero) for e in range(4)], axis=0
    )
    first = jnp.dot(table[...], weight, preferred_element_type=F32)
    sums = []
    for field in range(6):
        total = jnp.zeros((8, width), F32)
        for z in range(8):
            row = 64 * field + 8 * z
            total = total + first[row : row + 8] * lag_z[z : z + 1]
        sums.append(total * lag_a)
    return [
        jnp.sum(3.0 * sums[3 + comp] + tau * sums[comp], axis=0, keepdims=True)
        for comp in range(3)
    ]


def gather(rel, codes, recvr, onehot):
    held = rel.shape[1]
    n_xs = len(codes)
    rel8 = jnp.broadcast_to(rel, (8, held))
    answers = recvr[...].reshape(4 * n_xs, SLOTS)
    spread = jnp.dot(
        jnp.concatenate([p.astype(BF16) for p in split3(answers)], axis=0),
        onehot[...],
        preferred_element_type=F32,
    )
    span = 4 * n_xs
    half = lax.broadcasted_iota(jnp.int32, (8, held), 0) < 4
    total = jnp.zeros((8, held), F32)
    for pair in range(n_xs // 2):
        rows = [spread[w * span + 8 * pair : w * span + 8 * pair + 8] for w in range(3)]
        code = jnp.where(half, codes[2 * pair], codes[2 * pair + 1])
        total = total + jnp.where(rel8 == code, rows[0] + rows[1] + rows[2], 0.0)
    total = total + pltpu.roll(total, 4, 0)
    return total[0:3]


def kernel(
    n_ax, n_xs,
    part_hbm, elem_hbm, ref_hbm, tau_hbm, vel_hbm, metric_hbm, const_hbm, bvel_hbm, coef_hbm,
    hist_hbm,
    fluid_hbm, bubble_ref,
    part_ref, elem_ref, ref_ref, tau_ref, vel_ref, metric_ref, const_ref, bvel_ref, coef_ref,
    hist_ref,
    fluid_ref, lhs, onehot, sendq, recvq, sendr, recvr, table, wsum, face_out, face_in, plane_out, plane_in,
    local_sem, q_send, q_recv, r_send, r_recv, h_send, h_recv,
):
    ax = lax.axis_index("ax")
    me = lax.axis_index("xs")
    held = part_ref.shape[1]
    (length_x, length_y, cores), offsets = peers_by_distance(n_xs)
    codes = [(dx * length_y + dy) * cores + core for dx, dy, core in offsets]

    loads = [
        pltpu.make_async_copy(source, target, local_sem.at[i])
        for i, (source, target) in enumerate(
            [
                (part_hbm, part_ref), (elem_hbm, elem_ref), (ref_hbm, ref_ref),
                (tau_hbm, tau_ref), (vel_hbm, vel_ref), (metric_hbm, metric_ref),
                (const_hbm, const_ref), (bvel_hbm, bvel_ref), (coef_hbm, coef_ref),
                (hist_hbm, hist_ref),
            ]
        )
    ]
    def wrap(place, length):
        return jnp.where(place >= length, place - length, place)

    here_x = lax.div(me, length_y * cores)
    here_y = lax.rem(lax.div(me, cores), length_y)
    here_core = lax.rem(me, cores)
    places_x = [wrap(here_x + d, length_x) * (length_y * cores) for d in range(length_x)]
    places_y = [wrap(here_y + d, length_y) * cores for d in range(length_y)]
    places_core = [wrap(here_core + d, cores) for d in range(cores)]

    def ahead(place):
        dx, dy, core = offsets[place]
        return places_x[dx] + places_y[dy] + places_core[core]

    def behind(place):
        dx, dy, core = offsets[place]
        return (
            places_x[(length_x - dx) % length_x]
            + places_y[(length_y - dy) % length_y]
            + places_core[(cores - core) % cores]
        )

    up, down = wrap(ax + 1, n_ax), wrap(ax + n_ax - 1, n_ax)
    left, right = wrap(me + n_xs - 1, n_xs), wrap(me + 1, n_xs)

    barrier = pltpu.get_barrier_semaphore()
    for other in (up, down):
        pl.semaphore_signal(barrier, inc=1, device_id=(other, me), device_id_type=MESH)
    for place in range(n_xs - 1, 0, -1):
        pl.semaphore_signal(barrier, inc=1, device_id=(ax, behind(place)), device_id_type=MESH)

    def query_copy(first, count, group, target):
        return pltpu.make_async_remote_copy(
            src_ref=sendq.at[pl.ds(first, count), pl.ds(0, 5)],
            dst_ref=recvq.at[pl.ds(first, count), pl.ds(0, 5)],
            send_sem=q_send,
            recv_sem=q_recv.at[group],
            device_id=(ax, target),
            device_id_type=MESH,
        )

    def answer_copy(tile, count, odd, target):
        return pltpu.make_async_remote_copy(
            src_ref=sendr.at[pl.ds(tile, count), pl.ds(4 * odd, 3)],
            dst_ref=recvr.at[pl.ds(tile, count), pl.ds(4 * odd, 3)],
            send_sem=r_send.at[odd],
            recv_sem=r_recv.at[odd],
            device_id=(ax, target),
            device_id_type=MESH,
        )

    def face_copy(side):
        return pltpu.make_async_remote_copy(
            src_ref=face_out.at[side],
            dst_ref=face_in.at[side],
            send_sem=h_send.at[side],
            recv_sem=h_recv.at[side],
            device_id=(ax, right if side == 0 else left),
            device_id_type=MESH,
        )

    def plane_copy(side):
        return pltpu.make_async_remote_copy(
            src_ref=plane_out.at[side],
            dst_ref=plane_in.at[side],
            send_sem=h_send.at[2 + side],
            recv_sem=h_recv.at[2 + side],
            device_id=(up if side == 0 else down, me),
            device_id_type=MESH,
        )

    for load in loads:
        load.start()

    for load in loads[0:4]:
        load.wait()
    part = part_ref[...]
    far_x = part // (length_y * cores) - here_x
    far_y = (part // cores) % length_y - here_y
    far_core = part % cores - here_core
    rel = (
        jnp.where(far_x < 0, far_x + length_x, far_x) * (length_y * cores)
        + jnp.where(far_y < 0, far_y + length_y, far_y) * cores
        + jnp.where(far_core < 0, far_core + cores, far_core)
    )
    ranked(rel, n_xs, onehot)
    coords = jnp.concatenate([ref_ref[...], tau_ref[...]], axis=0)
    dispatch(rel, codes, coords, elem_ref[...].astype(F32), lhs, onehot, sendq, recvq)
    for load in loads[4:7]:
        load.wait()
    advection(vel_ref, metric_ref, const_ref, table, wsum)
    azimuth_pairs(wsum, face_out)
    pl.semaphore_wait(barrier, n_xs + 1)
    for place in range(n_xs - 1, 0, -1):
        query_copy(place, 1, place // GROUP, ahead(place)).start()
    for side in range(2):
        face_copy(side).start()

    groups = n_xs // GROUP
    middle = groups // 4
    order = list(range(middle, groups - 3))
    order += [g for g in range(groups - 1, -1, -1) if g not in order]
    for turn, group in enumerate(order):
        if turn == min(3, groups - 1):
            for side in range(2):
                face_copy(side).wait()
            add_faces(wsum, face_in, plane_out)
            for side in range(2):
                plane_copy(side).start()
        first = GROUP * group
        skip = 1 if group == 0 else 0
        query_copy(first + skip, GROUP - skip, group, me).wait_recv()
        sources = [recvq[first + i] for i in range(GROUP)]
        values = interpolate(jnp.concatenate(sources, axis=1), const_ref, table)
        for i in range(GROUP):
            place = first + i
            lanes = slice(SLOTS * i, SLOTS * (i + 1))
            target = sendr if place > 0 else recvr
            for comp in range(3):
                row = 4 * (place % 2) + comp
                target[place // 2, row : row + 1, :] = values[comp][:, lanes]
            if place > 0:
                answer_copy(place // 2, 1, place % 2, behind(place)).start()

    for load in loads[7:]:
        load.wait()
    quad = jnp.concatenate(
        [const_ref[ROW_QUAD + 8 * comp : ROW_QUAD + 8 * comp + 8, :] for comp in range(3)], axis=1
    )
    quad = jnp.concatenate([quad, jnp.zeros_like(quad)], axis=0).astype(BF16)
    basset = jnp.dot(quad, hist_ref[...], preferred_element_type=F32)[0:3]
    local = coef_ref[...] * basset - tau_ref[...] * bvel_ref[...]

    for side in range(2):
        plane_copy(side).wait()
    fluid_finish(wsum, plane_in, fluid_ref)
    store_fluid = pltpu.make_async_copy(fluid_ref, fluid_hbm, local_sem.at[len(loads)])
    store_fluid.start()

    query_copy(1, n_xs - 1, 0, me).wait_send()
    answer_copy(1, n_xs // 2 - 1, 0, me).wait()
    answer_copy(0, n_xs // 2, 1, me).wait()
    bubble_ref[...] = gather(rel, codes, recvr, onehot) + local
    store_fluid.wait()


def store(fluid_in, bubble_in, fluid_out, bubble_out, fluid_ref, bubble_ref, in_sems, out_sems):
    pieces = [(fluid_in.at[c], fluid_ref.at[c], fluid_out.at[c]) for c in range(3)]
    pieces.append((bubble_in, bubble_ref, bubble_out))
    reads = [pltpu.make_async_copy(p[0], p[1], in_sems.at[i]) for i, p in enumerate(pieces)]
    writes = [pltpu.make_async_copy(p[1], p[2], out_sems.at[i]) for i, p in enumerate(pieces)]
    for read in reads:
        read.start()
    for read, write in zip(reads, writes):
        read.wait()
        write.start()
    for write in writes:
        write.wait()


def shards(
    velocity, metric, bubble_part, bubble_elem, bubble_ref, bubble_vel, inv_tau,
    basset_coef, history,
):
    n_ax, n_xs = lax.axis_size("ax"), lax.axis_size("xs")
    held = bubble_part.shape[0]
    steps = history.shape[0]
    _, length_z, length_a, length_r = velocity.shape
    vmem = pl.BlockSpec(memory_space=pltpu.VMEM)
    anywhere = pl.BlockSpec(memory_space=pl.ANY)
    dma = pltpu.SemaphoreType.DMA
    outputs = (
        jax.ShapeDtypeStruct(velocity.shape, F32),
        jax.ShapeDtypeStruct((3, held), F32),
    )
    operands = [
        bubble_part.reshape(1, held),
        bubble_elem.reshape(1, held),
        bubble_ref,
        inv_tau.reshape(1, held),
        velocity,
        metric.reshape(3, length_a // 8, length_r // 8),
        jnp.asarray(constant_table(steps)),
        bubble_vel,
        basset_coef.reshape(1, held),
        history.transpose(1, 0, 2).reshape(3 * steps, held),
    ]
    results = pl.pallas_call(
        functools.partial(kernel, n_ax, n_xs),
        out_shape=outputs,
        in_specs=[anywhere] * len(operands),
        out_specs=(anywhere, vmem),
        scratch_shapes=[pltpu.VMEM(o.shape, o.dtype) for o in operands]
        + [
            pltpu.VMEM(velocity.shape, F32),
            pltpu.VMEM((16 * n_xs, held), BF16),
            pltpu.VMEM((SLOTS, held), BF16),
            pltpu.VMEM((n_xs, 8, SLOTS), F32),
            pltpu.VMEM((n_xs, 8, SLOTS), F32),
            pltpu.VMEM((n_xs // 2, 8, SLOTS), F32),
            pltpu.VMEM((n_xs // 2, 8, SLOTS), F32),
            pltpu.VMEM((6 * 64, 4 * length_r), BF16),
            pltpu.VMEM((4, length_z, length_a, length_r), F32),
            pltpu.VMEM((2, 4, length_z, length_r), F32),
            pltpu.VMEM((2, 4, length_z, length_r), F32),
            pltpu.VMEM((2, 4, length_a, length_r), F32),
            pltpu.VMEM((2, 4, length_a, length_r), F32),
            dma((len(operands) + 1,)),
            dma,
            dma((n_xs // GROUP,)),
            dma((2,)),
            dma((2,)),
            dma((4,)),
            dma((4,)),
        ],
        compiler_params=pltpu.CompilerParams(
            collective_id=0, has_side_effects=True, vmem_limit_bytes=56 * 1024 * 1024
        ),
    )(*operands)
    return pl.pallas_call(
        store,
        out_shape=outputs,
        in_specs=[anywhere, anywhere],
        out_specs=(anywhere, anywhere),
        scratch_shapes=[pltpu.VMEM(o.shape, o.dtype) for o in outputs] + [dma((4,)), dma((4,))],
        compiler_params=pltpu.CompilerParams(vmem_limit_bytes=56 * 1024 * 1024),
    )(*results)


def solution(mesh):
    return jax.shard_map(
        shards,
        mesh=mesh,
        in_specs=(
            P(None, "ax", "xs", None),
            P(None, "ax", "xs", None),
            P(("ax", "xs")),
            P(("ax", "xs")),
            P(None, ("ax", "xs")),
            P(None, ("ax", "xs")),
            P(("ax", "xs")),
            P(("ax", "xs")),
            P(None, None, ("ax", "xs")),
        ),
        out_specs=(P(None, "ax", "xs", None), P(None, ("ax", "xs"))),
        check_vma=False,
    )
```

```python
import functools

import jax
import jax.numpy as jnp
import numpy as np
from jax import lax
from jax.experimental import pallas as pl
from jax.experimental.pallas import tpu as pltpu
from jax.sharding import PartitionSpec as P

GLL_POINTS = (
    -1.0,
    -0.8717401485096066,
    -0.5917001814331423,
    -0.2092992179024789,
    0.2092992179024789,
    0.5917001814331423,
    0.8717401485096066,
    1.0,
)
GLL_WEIGHTS = (
    0.03571428571428571,
    0.21070422714350603,
    0.34112269248350435,
    0.4124587946587039,
    0.4124587946587039,
    0.34112269248350435,
    0.21070422714350603,
    0.03571428571428571,
)
SLOTS = 128
GROUP = 4
MESH = pl.DeviceIdType.MESH
F32 = jnp.float32
BF16 = jnp.bfloat16


def derivative_matrix():
    points = np.array(GLL_POINTS)
    identity = np.eye(8)
    spread = points[:, None] - points[None, :] + identity
    products = np.prod(spread, axis=1)
    matrix = products[:, None] / products[None, :] / spread
    off_diagonal = matrix * (1.0 - identity)
    return off_diagonal - identity * off_diagonal.sum(axis=1)[:, None]


DMAT = derivative_matrix()

ROW_POINT = 0
ROW_NORM = 8
ROW_ROLL = 16
ROW_WEIGHT = 80
ROW_RADIAL = 112
ROW_QUAD = 240


def constant_table(steps):
    points = np.array(GLL_POINTS)
    weights = np.array(GLL_WEIGHTS)
    rows = [np.repeat(points[:, None], 128, axis=1)]
    spread = points[:, None] - points[None, :] + np.eye(8)
    rows.append(np.repeat((1.0 / np.prod(spread, axis=1))[:, None], 128, axis=1))
    for shift in range(8):
        coef = np.array([DMAT[i, (i - shift) % 8] for i in range(8)])
        rows.append(np.repeat(coef[:, None], 128, axis=1))
    rows.append(np.tile(weights, 4)[:, None] * np.tile(weights, 16)[None, :])
    rows.append(np.kron(np.eye(16), DMAT.T))
    rows += quadrature_rows(steps)
    return np.concatenate(rows, axis=0).astype(np.float32)


def quadrature_rows(length):
    steps = np.arange(length, dtype=np.float32)
    quad = np.sqrt(steps + np.float32(1.0)) - np.sqrt(steps)
    rows = np.zeros((3, 8, length), np.float32)
    for comp in range(3):
        rows[comp, comp] = quad
    return list(rows)


def peers_by_distance(n_xs):
    length_x, length_y, cores = {32: (4, 4, 2), 4: (2, 1, 2)}[n_xs]
    offsets = [
        (dx, dy, core)
        for dx in range(length_x)
        for dy in range(length_y)
        for core in range(cores)
    ]

    def distance(offset):
        return min(offset[0], length_x - offset[0]) + min(offset[1], length_y - offset[1])

    return (length_x, length_y, cores), sorted(offsets, key=distance)


def split3(values):
    high = values.astype(BF16).astype(F32)
    rest = values - high
    mid = rest.astype(BF16).astype(F32)
    return high, mid, rest - mid


def ranked(rel, n_xs, onehot):
    held = rel.shape[1]
    member = (
        jnp.broadcast_to(rel, (n_xs, held))
        == lax.broadcasted_iota(jnp.int32, (n_xs, held), 0)
    ).astype(F32)
    chunks = held // 128
    pieces = [member[:, c * 128 : (c + 1) * 128] for c in range(chunks)]
    stacked = jnp.concatenate(pieces, axis=0).astype(BF16)
    before = (
        lax.broadcasted_iota(jnp.int32, (128, 128), 0)
        < lax.broadcasted_iota(jnp.int32, (128, 128), 1)
    ).astype(F32).astype(BF16)
    counts = jnp.dot(stacked, before, preferred_element_type=F32)
    totals = jnp.dot(stacked, jnp.ones((128, 128), BF16), preferred_element_type=F32)
    carry = jnp.zeros((n_xs, 128), F32)
    ranks = []
    for c in range(chunks):
        rows = slice(c * n_xs, (c + 1) * n_xs)
        ranks.append(jnp.sum(pieces[c] * (counts[rows] + carry), axis=0, keepdims=True))
        carry = carry + totals[rows]
    rank = jnp.concatenate(ranks, axis=1).astype(jnp.int32)
    onehot[...] = (
        jnp.broadcast_to(rank, (SLOTS, held))
        == lax.broadcasted_iota(jnp.int32, (SLOTS, held), 0)
    ).astype(F32).astype(BF16)


def dispatch(rel, codes, coords, elem, lhs, onehot, sendq, recvq):
    held = rel.shape[1]
    high, mid, low = split3(coords)
    packed = jnp.concatenate(
        [high, elem, jnp.zeros((3, held), F32), mid, low], axis=0
    ).astype(BF16)
    rel16 = jnp.broadcast_to(rel, (16, held))
    zero = jnp.zeros((16, held), BF16)
    n_xs = len(codes)
    for place, code in enumerate(codes):
        lhs[16 * place : 16 * place + 16, :] = jnp.where(rel16 == code, packed, zero)
    slots = lax.dot_general(
        lhs[...], onehot[...], (((1,), (1,)), ((), ())), preferred_element_type=F32
    ).reshape(n_xs, 2, 8, SLOTS)
    rest = slots[:, 1]
    rest = rest + pltpu.roll(rest, 4, 1)
    row = lax.broadcasted_iota(jnp.int32, (n_xs, 8, SLOTS), 1)
    slots = slots[:, 0] + jnp.where(row < 4, rest, 0.0)
    sendq[...] = slots
    recvq[0] = slots[0]


def advection(vel_ref, metric_ref, const_ref, table, wsum):
    vel = vel_ref[...]
    length_a, length_r = vel.shape[2], vel.shape[3]
    nodes = 8 * length_a
    grad_r = jnp.dot(
        vel.reshape(3 * nodes, length_r),
        const_ref[ROW_RADIAL : ROW_RADIAL + 128, :],
        preferred_element_type=F32,
        precision=lax.Precision.HIGHEST,
    ).reshape(vel.shape)
    spread = (
        lax.broadcasted_iota(jnp.int32, (length_r // 8, length_r), 1) // 8
        == lax.broadcasted_iota(jnp.int32, (length_r // 8, length_r), 0)
    ).astype(F32)
    scale = []
    for factor in range(3):
        rows = jnp.dot(
            metric_ref[factor], spread, preferred_element_type=F32, precision=lax.Precision.HIGHEST
        )
        scale.append(
            jnp.concatenate(
                [
                    jnp.broadcast_to(rows[e : e + 1], (8, length_r))
                    for e in range(length_a // 8)
                ],
                axis=0,
            )
        )
    inverse = const_ref[ROW_WEIGHT : ROW_WEIGHT + 32, :] / (scale[0] * scale[1] * scale[2])
    lane = lax.broadcasted_iota(jnp.int32, (4, length_a, length_r), 2)
    upper = (lane % 8 == 7) & (lane < length_r - 1)
    lower = (lane % 8 == 0) & (lane > 0)
    for z in range(8):
        here = vel[:, z]
        grad_z = sum(float(DMAT[z, j]) * vel[:, j] for j in range(8) if abs(DMAT[z, j]) > 1e-9)
        groups = here.reshape(3 * length_a // 8, 8, length_r)
        grad_a = const_ref[ROW_ROLL : ROW_ROLL + 8, :] * groups
        for shift in range(1, 8):
            coef = const_ref[ROW_ROLL + 8 * shift : ROW_ROLL + 8 * shift + 8, :]
            grad_a = grad_a + coef * pltpu.roll(groups, shift, 1)
        grad_a = grad_a.reshape(here.shape)
        advect = (
            (here[0] * scale[0])[None] * grad_z
            + (here[1] * scale[1])[None] * grad_a
            + (here[2] * scale[2])[None] * grad_r[:, z]
        )
        fields = [here[0], here[1], here[2], advect[0], advect[1], advect[2]]
        if z % 2 == 1:
            for field in range(6):
                for element in range(length_a // 8):
                    rows = slice(8 * element, 8 * element + 8)
                    pair = jnp.concatenate([earlier[field][rows], fields[field][rows]], axis=0)
                    table[
                        64 * field + 8 * (z - 1) : 64 * field + 8 * (z + 1),
                        length_r * element : length_r * (element + 1),
                    ] = pair.astype(BF16)
        earlier = fields
        mass = GLL_WEIGHTS[z] * inverse
        weighted = jnp.concatenate([mass[None] * advect, mass[None]], axis=0)
        after = pltpu.roll(weighted, length_r - 1, 2)
        prior = pltpu.roll(weighted, 1, 2)
        wsum[:, z] = weighted + jnp.where(upper, after, jnp.where(lower, prior, 0.0))


def azimuth_pairs(wsum, face_out):
    length_a = wsum.shape[2]
    for edge in range(8, length_a, 8):
        both = wsum[:, :, edge - 1 : edge, :] + wsum[:, :, edge : edge + 1, :]
        wsum[:, :, edge - 1 : edge, :] = both
        wsum[:, :, edge : edge + 1, :] = both
    for z in range(8):
        face_out[0, :, z : z + 1, :] = wsum[:, z, length_a - 1 : length_a, :]
        face_out[1, :, z : z + 1, :] = wsum[:, z, 0:1, :]


def add_faces(wsum, face_in, plane_out):
    length_a = wsum.shape[2]
    last = slice(length_a - 1, length_a)
    for z in range(8):
        wsum[:, z, 0:1, :] = wsum[:, z, 0:1, :] + face_in[0, :, z : z + 1, :]
        wsum[:, z, last, :] = wsum[:, z, last, :] + face_in[1, :, z : z + 1, :]
    plane_out[0] = wsum[:, 7]
    plane_out[1] = wsum[:, 0]


def fluid_finish(wsum, plane_in, fluid_ref):
    for z in range(8):
        total = wsum[:, z]
        if z == 0:
            total = total + plane_in[0]
        if z == 7:
            total = total + plane_in[1]
        fluid_ref[:, z] = total[0:3] * (-1.0 / total[3:4])


def interpolate(both, const_ref, table):
    width = both.shape[1]
    point = jnp.concatenate([const_ref[ROW_POINT : ROW_POINT + 8, :]] * (width // 128), axis=1)
    norm = jnp.concatenate([const_ref[ROW_NORM : ROW_NORM + 8, :]] * (width // 128), axis=1)

    def lagrange(row):
        diff = row - point
        one = pltpu.roll(diff, 1, 0)
        two = one * pltpu.roll(one, 1, 0)
        four = two * pltpu.roll(two, 2, 0)
        rest = four * pltpu.roll(two, 4, 0) * pltpu.roll(one, 6, 0)
        return (rest * norm).astype(BF16).astype(F32)

    lag_z = lagrange(both[0:1])
    lag_a = lagrange(both[1:2])
    lag_r = lagrange(both[2:3])
    tau = both[3:4]
    element = both[4:5].astype(jnp.int32)
    radial = jnp.broadcast_to(element & 15, (8, width))
    azimuth = jnp.broadcast_to((element >> 4) & 3, (128, width))
    weight_r = jnp.concatenate(
        [jnp.where(radial == e, lag_r, 0.0) for e in range(16)], axis=0
    ).astype(BF16)
    zero = jnp.zeros_like(weight_r)
    weight = jnp.concatenate(
        [jnp.where(azimuth == e, weight_r, zero) for e in range(4)], axis=0
    )
    first = jnp.dot(table[...], weight, preferred_element_type=F32)
    sums = []
    for field in range(6):
        total = jnp.zeros((8, width), F32)
        for z in range(8):
            row = 64 * field + 8 * z
            total = total + first[row : row + 8] * lag_z[z : z + 1]
        sums.append(total * lag_a)
    return [
        jnp.sum(3.0 * sums[3 + comp] + tau * sums[comp], axis=0, keepdims=True)
        for comp in range(3)
    ]


def gather(rel, codes, recvr, onehot):
    held = rel.shape[1]
    n_xs = len(codes)
    rel8 = jnp.broadcast_to(rel, (8, held))
    answers = recvr[...].reshape(4 * n_xs, SLOTS)
    spread = jnp.dot(
        jnp.concatenate([p.astype(BF16) for p in split3(answers)], axis=0),
        onehot[...],
        preferred_element_type=F32,
    )
    span = 4 * n_xs
    half = lax.broadcasted_iota(jnp.int32, (8, held), 0) < 4
    total = jnp.zeros((8, held), F32)
    for pair in range(n_xs // 2):
        rows = [spread[w * span + 8 * pair : w * span + 8 * pair + 8] for w in range(3)]
        code = jnp.where(half, codes[2 * pair], codes[2 * pair + 1])
        total = total + jnp.where(rel8 == code, rows[0] + rows[1] + rows[2], 0.0)
    total = total + pltpu.roll(total, 4, 0)
    return total[0:3]


def kernel(
    n_ax, n_xs,
    part_hbm, elem_hbm, ref_hbm, tau_hbm, vel_hbm, metric_hbm, const_hbm, bvel_hbm, coef_hbm,
    hist_hbm,
    fluid_hbm, bubble_ref,
    part_ref, elem_ref, ref_ref, tau_ref, vel_ref, metric_ref, const_ref, bvel_ref, coef_ref,
    hist_ref,
    fluid_ref, lhs, onehot, sendq, recvq, sendr, recvr, table, wsum, face_out, face_in, plane_out, plane_in,
    local_sem, q_send, q_recv, r_send, r_recv, h_send, h_recv,
):
    ax = lax.axis_index("ax")
    me = lax.axis_index("xs")
    held = part_ref.shape[1]
    (length_x, length_y, cores), offsets = peers_by_distance(n_xs)
    codes = [(dx * length_y + dy) * cores + core for dx, dy, core in offsets]

    loads = [
        pltpu.make_async_copy(source, target, local_sem.at[i])
        for i, (source, target) in enumerate(
            [
                (part_hbm, part_ref), (elem_hbm, elem_ref), (ref_hbm, ref_ref),
                (tau_hbm, tau_ref), (vel_hbm, vel_ref), (metric_hbm, metric_ref),
                (const_hbm, const_ref), (bvel_hbm, bvel_ref), (coef_hbm, coef_ref),
                (hist_hbm, hist_ref),
            ]
        )
    ]
    def wrap(place, length):
        return jnp.where(place >= length, place - length, place)

    here_x = lax.div(me, length_y * cores)
    here_y = lax.rem(lax.div(me, cores), length_y)
    here_core = lax.rem(me, cores)
    places_x = [wrap(here_x + d, length_x) * (length_y * cores) for d in range(length_x)]
    places_y = [wrap(here_y + d, length_y) * cores for d in range(length_y)]
    places_core = [wrap(here_core + d, cores) for d in range(cores)]

    def ahead(place):
        dx, dy, core = offsets[place]
        return places_x[dx] + places_y[dy] + places_core[core]

    def behind(place):
        dx, dy, core = offsets[place]
        return (
            places_x[(length_x - dx) % length_x]
            + places_y[(length_y - dy) % length_y]
            + places_core[(cores - core) % cores]
        )

    up, down = wrap(ax + 1, n_ax), wrap(ax + n_ax - 1, n_ax)
    left, right = wrap(me + n_xs - 1, n_xs), wrap(me + 1, n_xs)

    barrier = pltpu.get_barrier_semaphore()
    for other in (up, down):
        pl.semaphore_signal(barrier, inc=1, device_id=(other, me), device_id_type=MESH)
    for place in range(n_xs - 1, 0, -1):
        pl.semaphore_signal(barrier, inc=1, device_id=(ax, behind(place)), device_id_type=MESH)

    def query_copy(first, count, group, target):
        return pltpu.make_async_remote_copy(
            src_ref=sendq.at[pl.ds(first, count), pl.ds(0, 5)],
            dst_ref=recvq.at[pl.ds(first, count), pl.ds(0, 5)],
            send_sem=q_send,
            recv_sem=q_recv.at[group],
            device_id=(ax, target),
            device_id_type=MESH,
        )

    def answer_copy(tile, count, odd, target):
        return pltpu.make_async_remote_copy(
            src_ref=sendr.at[pl.ds(tile, count), pl.ds(4 * odd, 3)],
            dst_ref=recvr.at[pl.ds(tile, count), pl.ds(4 * odd, 3)],
            send_sem=r_send.at[odd],
            recv_sem=r_recv.at[odd],
            device_id=(ax, target),
            device_id_type=MESH,
        )

    def face_copy(side):
        return pltpu.make_async_remote_copy(
            src_ref=face_out.at[side],
            dst_ref=face_in.at[side],
            send_sem=h_send.at[side],
            recv_sem=h_recv.at[side],
            device_id=(ax, right if side == 0 else left),
            device_id_type=MESH,
        )

    def plane_copy(side):
        return pltpu.make_async_remote_copy(
            src_ref=plane_out.at[side],
            dst_ref=plane_in.at[side],
            send_sem=h_send.at[2 + side],
            recv_sem=h_recv.at[2 + side],
            device_id=(up if side == 0 else down, me),
            device_id_type=MESH,
        )

    for load in loads:
        load.start()

    for load in loads[0:4]:
        load.wait()
    part = part_ref[...]
    far_x = part // (length_y * cores) - here_x
    far_y = (part // cores) % length_y - here_y
    far_core = part % cores - here_core
    rel = (
        jnp.where(far_x < 0, far_x + length_x, far_x) * (length_y * cores)
        + jnp.where(far_y < 0, far_y + length_y, far_y) * cores
        + jnp.where(far_core < 0, far_core + cores, far_core)
    )
    ranked(rel, n_xs, onehot)
    coords = jnp.concatenate([ref_ref[...], tau_ref[...]], axis=0)
    dispatch(rel, codes, coords, elem_ref[...].astype(F32), lhs, onehot, sendq, recvq)
    pl.semaphore_wait(barrier, n_xs + 1)
    for place in range(n_xs - 1, 0, -1):
        query_copy(place, 1, place // GROUP, ahead(place)).start()
    for load in loads[4:7]:
        load.wait()
    advection(vel_ref, metric_ref, const_ref, table, wsum)
    azimuth_pairs(wsum, face_out)
    for side in range(2):
        face_copy(side).start()

    groups = n_xs // GROUP
    middle = groups // 4
    order = list(range(middle, groups - 4))
    order += [g for g in range(groups - 1, -1, -1) if g not in order]
    for turn, group in enumerate(order):
        if turn == min(3, groups - 1):
            for side in range(2):
                face_copy(side).wait()
            add_faces(wsum, face_in, plane_out)
            for side in range(2):
                plane_copy(side).start()
        first = GROUP * group
        skip = 1 if group == 0 else 0
        query_copy(first + skip, GROUP - skip, group, me).wait_recv()
        sources = [recvq[first + i] for i in range(GROUP)]
        values = interpolate(jnp.concatenate(sources, axis=1), const_ref, table)
        for i in range(GROUP):
            place = first + i
            lanes = slice(SLOTS * i, SLOTS * (i + 1))
            target = sendr if place > 0 else recvr
            for comp in range(3):
                row = 4 * (place % 2) + comp
                target[place // 2, row : row + 1, :] = values[comp][:, lanes]
            if place > 0:
                answer_copy(place // 2, 1, place % 2, behind(place)).start()

    for load in loads[7:]:
        load.wait()
    quad = jnp.concatenate(
        [const_ref[ROW_QUAD + 8 * comp : ROW_QUAD + 8 * comp + 8, :] for comp in range(3)], axis=1
    )
    quad = jnp.concatenate([quad, jnp.zeros_like(quad)], axis=0).astype(BF16)
    basset = jnp.dot(quad, hist_ref[...], preferred_element_type=F32)[0:3]
    local = coef_ref[...] * basset - tau_ref[...] * bvel_ref[...]

    for side in range(2):
        plane_copy(side).wait()
    fluid_finish(wsum, plane_in, fluid_ref)
    store_fluid = pltpu.make_async_copy(fluid_ref, fluid_hbm, local_sem.at[len(loads)])
    store_fluid.start()

    query_copy(1, n_xs - 1, 0, me).wait_send()
    answer_copy(1, n_xs // 2 - 1, 0, me).wait()
    answer_copy(0, n_xs // 2, 1, me).wait()
    bubble_ref[...] = gather(rel, codes, recvr, onehot) + local
    store_fluid.wait()


def store(fluid_in, bubble_in, fluid_out, bubble_out, fluid_ref, bubble_ref, in_sems, out_sems):
    pieces = [(fluid_in.at[c], fluid_ref.at[c], fluid_out.at[c]) for c in range(3)]
    pieces.append((bubble_in, bubble_ref, bubble_out))
    reads = [pltpu.make_async_copy(p[0], p[1], in_sems.at[i]) for i, p in enumerate(pieces)]
    writes = [pltpu.make_async_copy(p[1], p[2], out_sems.at[i]) for i, p in enumerate(pieces)]
    for read in reads:
        read.start()
    for read, write in zip(reads, writes):
        read.wait()
        write.start()
    for write in writes:
        write.wait()


def shards(
    velocity, metric, bubble_part, bubble_elem, bubble_ref, bubble_vel, inv_tau,
    basset_coef, history,
):
    n_ax, n_xs = lax.axis_size("ax"), lax.axis_size("xs")
    held = bubble_part.shape[0]
    steps = history.shape[0]
    _, length_z, length_a, length_r = velocity.shape
    vmem = pl.BlockSpec(memory_space=pltpu.VMEM)
    anywhere = pl.BlockSpec(memory_space=pl.ANY)
    dma = pltpu.SemaphoreType.DMA
    outputs = (
        jax.ShapeDtypeStruct(velocity.shape, F32),
        jax.ShapeDtypeStruct((3, held), F32),
    )
    operands = [
        bubble_part.reshape(1, held),
        bubble_elem.reshape(1, held),
        bubble_ref,
        inv_tau.reshape(1, held),
        velocity,
        metric.reshape(3, length_a // 8, length_r // 8),
        jnp.asarray(constant_table(steps)),
        bubble_vel,
        basset_coef.reshape(1, held),
        history.transpose(1, 0, 2).reshape(3 * steps, held),
    ]
    results = pl.pallas_call(
        functools.partial(kernel, n_ax, n_xs),
        out_shape=outputs,
        in_specs=[anywhere] * len(operands),
        out_specs=(anywhere, vmem),
        scratch_shapes=[pltpu.VMEM(o.shape, o.dtype) for o in operands]
        + [
            pltpu.VMEM(velocity.shape, F32),
            pltpu.VMEM((16 * n_xs, held), BF16),
            pltpu.VMEM((SLOTS, held), BF16),
            pltpu.VMEM((n_xs, 8, SLOTS), F32),
            pltpu.VMEM((n_xs, 8, SLOTS), F32),
            pltpu.VMEM((n_xs // 2, 8, SLOTS), F32),
            pltpu.VMEM((n_xs // 2, 8, SLOTS), F32),
            pltpu.VMEM((6 * 64, 4 * length_r), BF16),
            pltpu.VMEM((4, length_z, length_a, length_r), F32),
            pltpu.VMEM((2, 4, length_z, length_r), F32),
            pltpu.VMEM((2, 4, length_z, length_r), F32),
            pltpu.VMEM((2, 4, length_a, length_r), F32),
            pltpu.VMEM((2, 4, length_a, length_r), F32),
            dma((len(operands) + 1,)),
            dma,
            dma((n_xs // GROUP,)),
            dma((2,)),
            dma((2,)),
            dma((4,)),
            dma((4,)),
        ],
        compiler_params=pltpu.CompilerParams(
            collective_id=0, has_side_effects=True, vmem_limit_bytes=56 * 1024 * 1024
        ),
    )(*operands)
    return pl.pallas_call(
        store,
        out_shape=outputs,
        in_specs=[anywhere, anywhere],
        out_specs=(anywhere, anywhere),
        scratch_shapes=[pltpu.VMEM(o.shape, o.dtype) for o in outputs] + [dma((4,)), dma((4,))],
        compiler_params=pltpu.CompilerParams(vmem_limit_bytes=56 * 1024 * 1024),
    )(*results)


def solution(mesh):
    return jax.shard_map(
        shards,
        mesh=mesh,
        in_specs=(
            P(None, "ax", "xs", None),
            P(None, "ax", "xs", None),
            P(("ax", "xs")),
            P(("ax", "xs")),
            P(None, ("ax", "xs")),
            P(None, ("ax", "xs")),
            P(("ax", "xs")),
            P(("ax", "xs")),
            P(None, None, ("ax", "xs")),
        ),
        out_specs=(P(None, "ax", "xs", None), P(None, ("ax", "xs"))),
        check_vma=False,
    )
```
